256 devices in a mesh: seq: 64 (over y, z_hi, x), cfg: 2 (over core), clip: 2 (over z_lo).
Axes of the slice: x: 4, y: 4, z: 8 (z_hi: 4, z_lo: 2; z = z_hi * 2 + z_lo), core: 2. Of those that a mesh axis runs over, the one named last changes fastest.
Arguments:
- queries: bfloat16 [2, 2, 2048, 2560], P(None, 'cfg', ('clip', 'seq')), parts along dimension 2, may hold values from -8 to 8
- fresh_kv: bfloat16 [2, 2, 2, 2048, 2560], P(None, 'cfg', None, ('clip', 'seq')), parts along dimension 3, may hold values from -8 to 8
- stale_kv: bfloat16 [2, 2, 2048, 2560], P('cfg', None, ('clip', 'seq')), parts along dimension 2, may hold values from -8 to 8
- timesteps: int32 [2], replicated, may hold values from 0 to 999
- guidance_index: int32 [1], replicated, may hold values from 0 to 11
Outputs:
- guided: bfloat16 [2, 2048, 2560], P(None, ('clip', 'seq'), 'cfg'), parts along dimension 1
The draws below stay inside these ranges and needn't reach their ends.
There are 2 independent parts, one for each index of `clip`. The reference program is written for one: setup_inputs(seed, part) draws one part's arguments, and reference() takes and returns one part's arrays. A program takes and returns all parts, laid end to end along the dimension named above; an argument that names none is the same for every part. Nothing has to cross between parts.
All inputs are finite; a program needn't handle non-finite values.
Results may differ from the reference program's by a relative error of at most 0.0065.
Values may be sent and summed in bfloat16 or wider, within the bound.
A program may use at most 128 MiB of HBM per device.

```python
import math
import jax
import jax.numpy as jnp
from jax import lax

HEADS = 20
HEAD_DIM = 128
TOK_DEV = 16
STEPS = 2
CHANNELS = 2560
SEQ_TOKENS = 1024
N_SEQ = 64


def draw_keys_values(key, lead):
    key = jax.random.fold_in(key, 11 + lead)
    shape = (lead, 2, SEQ_TOKENS, CHANNELS)
    values = jnp.clip(jax.random.normal(key, shape, dtype=jnp.float32), -6.0, 6.0)
    return values


def draw_queries(key, part):
    key = jax.random.fold_in(key, 3)
    values = jnp.clip(2.0 * jax.random.normal(key, (STEPS, 2, SEQ_TOKENS, CHANNELS), dtype=jnp.float32), -8.0, 8.0)
    return values.astype(jnp.bfloat16)


def draw_fresh_kv(key, part):
    stacked = draw_keys_values(key, STEPS * 2)
    return stacked.reshape(STEPS, 2, 2, SEQ_TOKENS, CHANNELS).astype(jnp.bfloat16)


def draw_stale_kv(key, part):
    return draw_keys_values(jax.random.fold_in(key, 5), 2).astype(jnp.bfloat16)


def setup_inputs(seed: int = 0, part: int = 0) -> dict:
    splits = jax.random.split(jax.random.key(seed), 6)
    part_splits = jax.random.split(jax.random.fold_in(splits[5], part), 6)
    queries = draw_queries(jax.random.fold_in(jax.random.fold_in(splits[5], part), 71), part)
    fresh_kv = draw_fresh_kv(jax.random.fold_in(jax.random.fold_in(splits[5], part), 71), part)
    stale_kv = draw_stale_kv(jax.random.fold_in(jax.random.fold_in(splits[5], part), 71), part)
    timesteps = jax.random.randint(splits[3], (STEPS,), 0, 1000).astype(jnp.int32)
    guidance_index = jax.random.randint(splits[4], (1,), 0, 12).astype(jnp.int32)
    return dict(queries=queries, fresh_kv=fresh_kv, stale_kv=stale_kv, timesteps=timesteps, guidance_index=guidance_index)


def head_attention(query_rows, key_rows, value_rows):
    count = query_rows.shape[0]
    total = key_rows.shape[0]
    query_heads = query_rows.reshape(count, HEADS, HEAD_DIM).astype(jnp.float32)
    key_heads = key_rows.reshape(total, HEADS, HEAD_DIM).astype(jnp.float32)
    value_heads = value_rows.reshape(total, HEADS, HEAD_DIM).astype(jnp.float32)
    scores = jnp.einsum('qhe,khe->qhk', query_heads, key_heads) / math.sqrt(HEAD_DIM)
    top_score = lax.optimization_barrier(jnp.max(scores, axis=-1, keepdims=True))
    weights = jnp.exp(scores - top_score)
    totals = lax.optimization_barrier(jnp.sum(weights, axis=-1))
    rounded = lax.optimization_barrier(weights.astype(jnp.bfloat16)).astype(jnp.float32)
    summed = jnp.einsum('qhk,khe->qhe', rounded, value_heads)
    return (summed / totals[..., None]).astype(jnp.bfloat16).reshape(count, CHANNELS)

def branch_attention(query_all, own_kv, remote_kv):
    blocks = jnp.arange(N_SEQ, dtype=jnp.int32)

    def one_block(block_no):
        first = (block_no * TOK_DEV).astype(jnp.int32)
        query_rows = lax.dynamic_slice_in_dim(query_all, first, TOK_DEV, 0)
        mine = lax.dynamic_slice_in_dim(own_kv, first, TOK_DEV, 1)
        merged = lax.dynamic_update_slice_in_dim(remote_kv, mine, first, 1)
        return head_attention(query_rows, merged[0], merged[1])
    result = lax.map(one_block, blocks)
    return result.reshape(N_SEQ * TOK_DEV, CHANNELS)

def reference(queries, fresh_kv, stale_kv, timesteps, guidance_index):
    scale = 1.0 + 0.5 * guidance_index[0].astype(jnp.float32)
    channel_ids = jnp.arange(CHANNELS, dtype=jnp.float32)
    frequency = jnp.exp(-math.log(1000.0) * channel_ids / CHANNELS)
    results = []
    for step_no in range(STEPS):
        if step_no == 0:
            remote = stale_kv
        else:
            remote = fresh_kv[step_no - 1]
        cond = branch_attention(queries[step_no, 0], fresh_kv[step_no, 0], remote[0]).astype(jnp.float32)
        uncond = branch_attention(queries[step_no, 1], fresh_kv[step_no, 1], remote[1]).astype(jnp.float32)
        gate = 1.0 + 0.5 * jnp.sin(timesteps[step_no].astype(jnp.float32) * frequency)
        results.append((gate[None, :] * (uncond + scale * (cond - uncond))).astype(jnp.bfloat16))
    return jnp.stack(results, axis=0)
```

```python
import functools
import math

import jax
import jax.numpy as jnp
from jax import lax
from jax.experimental import pallas as pl
from jax.experimental.pallas import tpu as pltpu
from jax.sharding import PartitionSpec as P

MESH = pl.DeviceIdType.MESH
HEAD_DIM = 128
HEADS = 20
HALF_HEADS = HEADS // 2
STEPS = 2
UNITS = STEPS * HEADS
TOK = 16
N_SEQ = 64
SEQ_TOKENS = TOK * N_SEQ
CHUNK_SLOTS = 16
CHUNK = CHUNK_SLOTS * TOK
N_CHUNKS = N_SEQ // CHUNK_SLOTS
BRANCH_SHIFT = N_SEQ - UNITS
SCORE_SCALE = 1.0 / math.sqrt(HEAD_DIM)
LOG2E = math.log2(math.e)
MASKED = -1e30


def shifted(place, slot, sign):
    dz, dx, dy = slot % 4, (slot // 4) % 4, slot // 16
    y, z, x = place // 16, (place // 4) % 4, place % 4
    y = (y + sign * dy + 4) % 4
    z = (z + sign * dz + 4) % 4
    x = (x + sign * dx + 4) % 4
    return (y * 4 + z) * 4 + x


def unit_of(place, branch):
    y, z, x = place // 16, (place // 4) % 4, place % 4
    rank = (((y - z + 4) % 4) * 4 + x) * 4 + z
    return rank - BRANCH_SHIFT * branch


def stacked_heads(rows):
    return jnp.concatenate(
        [rows[:, h * HEAD_DIM : (h + 1) * HEAD_DIM] for h in range(HEADS)], axis=0
    )


def with_ones(values):
    return jnp.concatenate([values, jnp.ones_like(values)], axis=1)


def kernel(
    ts_ref, gi_ref, q_hbm, fresh_hbm, stale_hbm, out_ref,
    q_src, kv_src, kv_rx, q_rx, scores_ref, o_buf, lse_buf, o_rx, lse_rx, own_all, own_fin,
    load_sem, kv_sem, q_sem, kv_send, q_send, o_send, lse_send, o_sem, lse_sem, own_send, own_sem,
):
    me = lax.axis_index("seq")
    branch = lax.axis_index("cfg")
    clip = lax.axis_index("clip")
    unit = unit_of(me, branch)
    has_unit = jnp.logical_and(unit >= 0, unit < UNITS)

    barrier = pltpu.get_barrier_semaphore()

    loads = [
        pltpu.make_async_copy(stale_hbm.at[0], kv_src.at[0], load_sem.at[0]),
        pltpu.make_async_copy(fresh_hbm.at[0, 0], kv_src.at[1], load_sem.at[1]),
        pltpu.make_async_copy(q_hbm.at[:, 0], q_src, load_sem.at[2]),
        pltpu.make_async_copy(fresh_hbm.at[1, 0], kv_src.at[2], load_sem.at[3]),
    ]
    for load in loads:
        load.start()

    pl.semaphore_signal(barrier, inc=1, device_id=(me, 1 - branch, clip), device_id_type=MESH)

    @pl.when(has_unit)
    def _():
        def greet(slot, carry):
            pl.semaphore_signal(
                barrier, inc=1, device_id=(shifted(me, slot, 1), branch, clip), device_id_type=MESH
            )
            return carry

        lax.fori_loop(1, N_SEQ, greet, 0)

    for load in loads:
        load.wait()

    @pl.when(has_unit)
    def _():
        pl.semaphore_wait(barrier, UNITS)

    @pl.when(jnp.logical_not(has_unit))
    def _():
        pl.semaphore_wait(barrier, UNITS + 1)

    def kv_block(u):
        return kv_src.at[u // HEADS, :, :, pl.ds(pl.multiple_of(u % HEADS * HEAD_DIM, HEAD_DIM), HEAD_DIM)]

    def q_block(u):
        return q_src.at[u // HEADS, :, pl.ds(pl.multiple_of(u % HEADS * HEAD_DIM, HEAD_DIM), HEAD_DIM)]

    def slot_rows(slot):
        return pl.ds(pl.multiple_of(slot * TOK, TOK), TOK)

    @pl.when(has_unit)
    def _():
        pltpu.make_async_copy(kv_block(unit), kv_rx.at[:, pl.ds(0, TOK), :], kv_sem).start()
        pltpu.make_async_copy(q_block(unit), q_rx.at[pl.ds(0, TOK), :], q_sem.at[0]).start()

    def send_kv(slot, carry):
        there = shifted(me, slot, -1)
        u = unit_of(there, branch)

        @pl.when(jnp.logical_and(u >= 0, u < UNITS))
        def _():
            pltpu.make_async_remote_copy(
                src_ref=kv_block(u),
                dst_ref=kv_rx.at[:, slot_rows(slot), :],
                send_sem=kv_send,
                recv_sem=kv_sem,
                device_id=(there, branch, clip),
                device_id_type=MESH,
            ).start()

        return carry

    lax.fori_loop(1, N_SEQ, send_kv, 0)

    def send_q(slot, carry):
        there = shifted(me, slot, -1)
        u = unit_of(there, branch)

        @pl.when(jnp.logical_and(u >= 0, u < UNITS))
        def _():
            pltpu.make_async_remote_copy(
                src_ref=q_block(u),
                dst_ref=q_rx.at[slot_rows(slot), :],
                send_sem=q_send,
                recv_sem=q_sem.at[slot // CHUNK_SLOTS],
                device_id=(there, branch, clip),
                device_id_type=MESH,
            ).start()

        return carry

    lax.fori_loop(1, N_SEQ, send_q, 0)

    rows = HEADS * TOK
    same_head = (
        lax.broadcasted_iota(jnp.int32, (rows, rows), 0) // TOK
        == lax.broadcasted_iota(jnp.int32, (rows, rows), 1) // TOK
    )
    for s in range(STEPS):
        scores = lax.dot_general(
            stacked_heads(q_src[s]),
            stacked_heads(kv_src[s + 1, 0]),
            (((1,), (1,)), ((), ())),
            preferred_element_type=jnp.float32,
        )
        scores = jnp.where(same_head, scores, MASKED)
        top = jnp.max(scores, axis=1, keepdims=True)
        weights = jnp.exp2((scores - top) * (SCORE_SCALE * LOG2E)).astype(jnp.bfloat16)
        summed = jnp.dot(
            weights, with_ones(stacked_heads(kv_src[s + 1, 1])), preferred_element_type=jnp.float32
        )
        totals = summed[:, HEAD_DIM:]
        own_all[:, s, 0] = (summed[:, :HEAD_DIM] / totals).reshape(2, rows // 2, HEAD_DIM)
        own_all[:, s, 1] = (top * SCORE_SCALE + jnp.log(totals)).reshape(2, rows // 2, HEAD_DIM)

    own_copy = pltpu.make_async_remote_copy(
        src_ref=own_all.at[1 - branch],
        dst_ref=own_fin.at[branch],
        send_sem=own_send,
        recv_sem=own_sem.at[0],
        device_id=(me, 1 - branch, clip),
        device_id_type=MESH,
    )
    own_copy.start()
    own_local = pltpu.make_async_copy(own_all.at[branch], own_fin.at[branch], own_sem.at[1])
    own_local.start()

    channel = (
        branch * (HALF_HEADS * HEAD_DIM)
        + lax.broadcasted_iota(jnp.int32, (HALF_HEADS, 1, HEAD_DIM), 0) * HEAD_DIM
        + lax.broadcasted_iota(jnp.int32, (HALF_HEADS, 1, HEAD_DIM), 2)
    ).astype(jnp.float32)
    frequency = jnp.exp(-math.log(1000.0) * channel / (HEADS * HEAD_DIM))
    gates = [
        1.0 + 0.5 * jnp.sin(ts_ref[s].astype(jnp.float32) * frequency) for s in range(STEPS)
    ]
    scale = 1.0 + 0.5 * gi_ref[0].astype(jnp.float32)

    head = unit % HEADS
    half = head // HALF_HEADS
    unit_step = unit // HEADS

    def send_out(slot, there):
        pltpu.make_async_remote_copy(
            src_ref=o_buf.at[slot_rows(slot), :],
            dst_ref=o_rx.at[branch, unit_step, head % HALF_HEADS],
            send_sem=o_send,
            recv_sem=o_sem,
            device_id=(there, half, clip),
            device_id_type=MESH,
        ).start()
        pltpu.make_async_remote_copy(
            src_ref=lse_buf.at[slot],
            dst_ref=lse_rx.at[branch, unit_step, head % HALF_HEADS],
            send_sem=lse_send,
            recv_sem=lse_sem,
            device_id=(there, half, clip),
            device_id_type=MESH,
        ).start()

    @pl.when(has_unit)
    def _():
        pltpu.make_async_copy(kv_rx, kv_rx, kv_sem).wait()
        same_patch = (
            lax.broadcasted_iota(jnp.int32, (CHUNK, CHUNK), 0) // TOK
            == lax.broadcasted_iota(jnp.int32, (CHUNK, CHUNK), 1) // TOK
        )
        lane_token = lax.broadcasted_iota(jnp.int32, (1, TOK, HEAD_DIM), 2) % TOK
        picked = lane_token == lax.broadcasted_iota(jnp.int32, (1, TOK, HEAD_DIM), 1)
        for c in range(N_CHUNKS):
            here = pl.ds(c * CHUNK, CHUNK)
            pltpu.make_async_copy(q_rx.at[here], q_rx.at[here], q_sem.at[c]).wait()
            scores_ref[...] = lax.dot_general(
                q_rx[here, :], kv_rx[0], (((1,), (1,)), ((), ())), preferred_element_type=jnp.float32
            )
            scores_ref[:, here] = jnp.where(same_patch, MASKED, scores_ref[:, here])
            scores = scores_ref[...]
            top = jnp.max(scores, axis=1, keepdims=True)
            weights = jnp.exp2((scores - top) * (SCORE_SCALE * LOG2E)).astype(jnp.bfloat16)
            summed = jnp.dot(weights, with_ones(kv_rx[1]), preferred_element_type=jnp.float32)
            totals = summed[:, HEAD_DIM:]
            o_buf[here, :] = (summed[:, :HEAD_DIM] / totals).astype(jnp.bfloat16)
            lse = (top * SCORE_SCALE + jnp.log(totals)).reshape(CHUNK_SLOTS, TOK, HEAD_DIM)
            lse_buf[pl.ds(c * CHUNK_SLOTS, CHUNK_SLOTS)] = jnp.sum(
                jnp.where(picked, lse, 0.0), axis=1, keepdims=True
            )
            if c == 0:

                @pl.when(half == branch)
                def _():
                    pltpu.make_async_copy(
                        o_buf.at[pl.ds(0, TOK), :], o_rx.at[branch, unit_step, head % HALF_HEADS], o_sem
                    ).start()
                    pltpu.make_async_copy(
                        lse_buf.at[0], lse_rx.at[branch, unit_step, head % HALF_HEADS], lse_sem
                    ).start()

                @pl.when(half != branch)
                def _():
                    send_out(0, me)

            def send_slot(slot, carry):
                send_out(slot, shifted(me, slot, 1))
                return carry

            lax.fori_loop(max(1, c * CHUNK_SLOTS), (c + 1) * CHUNK_SLOTS, send_slot, 0)

    own_copy.wait_recv()
    own_local.wait()
    pltpu.make_async_copy(lse_rx, lse_rx, lse_sem).wait()
    pltpu.make_async_copy(o_rx, o_rx, o_sem).wait()

    token = lax.broadcasted_iota(jnp.int32, (1, TOK, HEAD_DIM), 1)
    lane = lax.broadcasted_iota(jnp.int32, (1, TOK, HEAD_DIM), 2)

    def attended(b, s):
        remote = o_rx[b, s].astype(jnp.float32)
        remote_lse = jnp.sum(jnp.where(token == lane, lse_rx[b, s], 0.0), axis=2, keepdims=True)
        own = own_fin[b, s, 0].reshape(HALF_HEADS, TOK, HEAD_DIM)
        own_lse = own_fin[b, s, 1].reshape(HALF_HEADS, TOK, HEAD_DIM)
        share = 1.0 / (1.0 + jnp.exp(own_lse - remote_lse))
        return own + share * (remote - own)

    for s in range(STEPS):
        cond = attended(0, s)
        uncond = attended(1, s)
        guided = (gates[s] * (uncond + scale * (cond - uncond))).astype(jnp.bfloat16)
        for h in range(HALF_HEADS):
            out_ref[s, :, h * HEAD_DIM : (h + 1) * HEAD_DIM] = guided[h]

    own_copy.wait_send()

    @pl.when(has_unit)
    def _():
        sent = pl.ds(0, (UNITS - 1) * TOK)
        pltpu.make_async_copy(kv_rx.at[:, sent, :], kv_rx.at[:, sent, :], kv_send).wait()
        pltpu.make_async_copy(q_rx.at[sent], q_rx.at[sent], q_send).wait()

        @pl.when(half == branch)
        def _():
            out_rows, lse_rows = pl.ds(TOK, SEQ_TOKENS - TOK), pl.ds(1, N_SEQ - 1)
            pltpu.make_async_copy(o_buf.at[out_rows], o_buf.at[out_rows], o_send).wait()
            pltpu.make_async_copy(lse_buf.at[lse_rows], lse_buf.at[lse_rows], lse_send).wait()

        @pl.when(half != branch)
        def _():
            pltpu.make_async_copy(o_buf, o_buf, o_send).wait()
            pltpu.make_async_copy(lse_buf, lse_buf, lse_send).wait()

    @pl.when(jnp.logical_not(has_unit))
    def _():
        sent = pl.ds(0, UNITS * TOK)
        pltpu.make_async_copy(kv_rx.at[:, sent, :], kv_rx.at[:, sent, :], kv_send).wait()
        pltpu.make_async_copy(q_rx.at[sent], q_rx.at[sent], q_send).wait()


def shards(queries, fresh_kv, stale_kv, timesteps, guidance_index):
    bf16, f32 = jnp.bfloat16, jnp.float32
    rows = HALF_HEADS * TOK
    dma = pltpu.SemaphoreType.DMA
    return pl.pallas_call(
        kernel,
        out_shape=jax.ShapeDtypeStruct((STEPS, TOK, HALF_HEADS * HEAD_DIM), bf16),
        in_specs=[pl.BlockSpec(memory_space=pltpu.SMEM)] * 2 + [pl.BlockSpec(memory_space=pl.ANY)] * 3,
        out_specs=pl.BlockSpec(memory_space=pltpu.VMEM),
        scratch_shapes=[
            pltpu.VMEM((STEPS, TOK, HEADS * HEAD_DIM), bf16),
            pltpu.VMEM((STEPS + 1, 2, TOK, HEADS * HEAD_DIM), bf16),
            pltpu.VMEM((2, SEQ_TOKENS, HEAD_DIM), bf16),
            pltpu.VMEM((SEQ_TOKENS, HEAD_DIM), bf16),
            pltpu.VMEM((CHUNK, SEQ_TOKENS), f32),
            pltpu.VMEM((SEQ_TOKENS, HEAD_DIM), bf16),
            pltpu.VMEM((N_SEQ, 1, HEAD_DIM), f32),
            pltpu.VMEM((2, STEPS, HALF_HEADS, TOK, HEAD_DIM), bf16),
            pltpu.VMEM((2, STEPS, HALF_HEADS, 1, HEAD_DIM), f32),
            pltpu.VMEM((2, STEPS, 2, rows, HEAD_DIM), f32),
            pltpu.VMEM((2, STEPS, 2, rows, HEAD_DIM), f32),
            dma((4,)), dma, dma((N_CHUNKS,)),
            dma, dma, dma, dma,
            dma, dma, dma, dma((2,)),
        ],
        compiler_params=pltpu.CompilerParams(
            collective_id=0, has_side_effects=True, vmem_limit_bytes=32 * 2**20
        ),
        name="patch_attention",
    )(timesteps, guidance_index, queries, fresh_kv, stale_kv)


def solution(mesh):
    in_specs = (
        P(None, "cfg", ("clip", "seq"), None),
        P(None, "cfg", None, ("clip", "seq"), None),
        P("cfg", None, ("clip", "seq"), None),
        P(),
        P(),
    )
    out_specs = P(None, ("clip", "seq"), "cfg")
    return jax.shard_map(shards, mesh=mesh, in_specs=in_specs, out_specs=out_specs, check_vma=False)
```

```python
import functools
import math

import jax
import jax.numpy as jnp
from jax import lax
from jax.experimental import pallas as pl
from jax.experimental.pallas import tpu as pltpu
from jax.sharding import PartitionSpec as P

MESH = pl.DeviceIdType.MESH
HEAD_DIM = 128
HEADS = 20
HALF_HEADS = HEADS // 2
STEPS = 2
UNITS = STEPS * HEADS
TOK = 16
N_SEQ = 64
SEQ_TOKENS = TOK * N_SEQ
CHUNK_SLOTS = 16
CHUNK = CHUNK_SLOTS * TOK
N_CHUNKS = N_SEQ // CHUNK_SLOTS
BRANCH_SHIFT = N_SEQ - UNITS
SCORE_SCALE = 1.0 / math.sqrt(HEAD_DIM)
LOG2E = math.log2(math.e)
MASKED = -1e30


PLANES = (2, 1, 3, 0)
SELF = N_SEQ - 1


def rank_of(place):
    y, z, x = place >> 4, (place >> 2) & 3, place & 3
    return ((y ^ z) << 4) + (x << 2) + z


def holds_unit(unit):
    return jnp.logical_and(unit >= 0, unit < UNITS)


def step_and_head(unit):
    step = (unit >= HEADS).astype(jnp.int32)
    return step, unit - step * HEADS


def far_to_near(k):
    return (0x36 >> (2 * k)) & 3


def for_slots(chunks, body):
    def across(i, carry):
        column = (far_to_near(i >> 2) << 4) + far_to_near(i & 3)
        for c in chunks:
            run = functools.partial(body, c, c * CHUNK_SLOTS + i, column + PLANES[c] * 4)
            if PLANES[c] == 0:
                pl.when(i < CHUNK_SLOTS - 1)(run)
            else:
                run()
        return carry

    lax.fori_loop(0, CHUNK_SLOTS, across, 0)


def stacked_heads(rows):
    return jnp.concatenate(
        [rows[:, h * HEAD_DIM : (h + 1) * HEAD_DIM] for h in range(HEADS)], axis=0
    )


def with_ones(values):
    return jnp.concatenate([values, jnp.ones_like(values)], axis=1)


def kernel(
    ts_hbm, gi_hbm, q_hbm, fresh_hbm, stale_hbm, out_ref,
    ts_ref, gi_ref, q_src, kv_src, kv_rx, q_rx, scores_ref, o_buf, lse_buf, o_rx, lse_rx, own_all, own_fin,
    load_sem, kv_sem, q_sem, kv_send, q_send, o_send, lse_send, o_sem, lse_sem, own_send, own_sem,
):
    me = lax.axis_index("seq")
    branch = lax.axis_index("cfg")
    clip = lax.axis_index("clip")
    my_rank = rank_of(me)
    first_rank = BRANCH_SHIFT * branch
    unit = my_rank - first_rank
    has_unit = holds_unit(unit)
    unit_step, head = step_and_head(unit)
    half = (head >= HALF_HEADS).astype(jnp.int32)
    half_head = head - half * HALF_HEADS

    barrier = pltpu.get_barrier_semaphore()

    loads = [
        pltpu.make_async_copy(stale_hbm.at[0], kv_src.at[0], load_sem.at[0]),
        pltpu.make_async_copy(fresh_hbm.at[0, 0], kv_src.at[1], load_sem.at[1]),
        pltpu.make_async_copy(q_hbm.at[:, 0], q_src, load_sem.at[2]),
        pltpu.make_async_copy(fresh_hbm.at[1, 0], kv_src.at[2], load_sem.at[3]),
        pltpu.make_async_copy(ts_hbm, ts_ref, load_sem.at[4]),
        pltpu.make_async_copy(gi_hbm, gi_ref, load_sem.at[5]),
    ]
    for load in loads:
        load.start()

    pl.semaphore_signal(barrier, inc=1, device_id=(me, 1 - branch, clip), device_id_type=MESH)

    @pl.when(has_unit)
    def _():
        def greet(chunk, slot, code):
            pl.semaphore_signal(
                barrier, inc=1, device_id=(me ^ code, branch, clip), device_id_type=MESH
            )

        for_slots((0,), greet)
        for_slots((1, 2, 3), greet)

    for load in loads[:3]:
        load.wait()
    pl.semaphore_wait(barrier, UNITS + 1 - has_unit.astype(jnp.int32))

    def kv_block(step, h):
        return kv_src.at[step, :, :, pl.ds(pl.multiple_of(h * HEAD_DIM, HEAD_DIM), HEAD_DIM)]

    def q_block(step, h):
        return q_src.at[step, :, pl.ds(pl.multiple_of(h * HEAD_DIM, HEAD_DIM), HEAD_DIM)]

    def slot_rows(slot):
        return pl.ds(pl.multiple_of(slot * TOK, TOK), TOK)

    def send_kv(chunk, slot, code):
        u = (my_rank ^ rank_of(code)) - first_rank

        @pl.when(holds_unit(u))
        def _():
            pltpu.make_async_remote_copy(
                src_ref=kv_block(*step_and_head(u)),
                dst_ref=kv_rx.at[:, slot_rows(slot), :],
                send_sem=kv_send,
                recv_sem=kv_sem,
                device_id=(me ^ code, branch, clip),
                device_id_type=MESH,
            ).start()

    def send_q(chunk, slot, code):
        u = (my_rank ^ rank_of(code)) - first_rank

        @pl.when(holds_unit(u))
        def _():
            pltpu.make_async_remote_copy(
                src_ref=q_block(*step_and_head(u)),
                dst_ref=q_rx.at[slot_rows(slot), :],
                send_sem=q_send,
                recv_sem=q_sem.at[chunk],
                device_id=(me ^ code, branch, clip),
                device_id_type=MESH,
            ).start()

    for_slots((0,), send_q)
    for_slots((0,), send_kv)
    for_slots((1, 2, 3), send_kv)
    for_slots((1, 2, 3), send_q)

    @pl.when(has_unit)
    def _():
        pltpu.make_async_copy(
            kv_block(unit_step, head), kv_rx.at[:, pl.ds(SELF * TOK, TOK), :], kv_sem
        ).start()
        pltpu.make_async_copy(
            q_block(unit_step, head), q_rx.at[pl.ds(SELF * TOK, TOK), :], q_sem.at[N_CHUNKS - 1]
        ).start()

    for load in loads[3:]:
        load.wait()

    rows = HEADS * TOK
    same_head = (
        lax.broadcasted_iota(jnp.int32, (rows, rows), 0) // TOK
        == lax.broadcasted_iota(jnp.int32, (rows, rows), 1) // TOK
    )
    for s in range(STEPS):
        scores = lax.dot_general(
            stacked_heads(q_src[s]),
            stacked_heads(kv_src[s + 1, 0]),
            (((1,), (1,)), ((), ())),
            preferred_element_type=jnp.float32,
        )
        scores = jnp.where(same_head, scores, MASKED)
        top = jnp.max(scores, axis=1, keepdims=True)
        weights = jnp.exp2((scores - top) * (SCORE_SCALE * LOG2E)).astype(jnp.bfloat16)
        summed = jnp.dot(
            weights, with_ones(stacked_heads(kv_src[s + 1, 1])), preferred_element_type=jnp.float32
        )
        totals = summed[:, HEAD_DIM:]
        own_all[:, s, 0] = (summed[:, :HEAD_DIM] / totals).reshape(2, rows // 2, HEAD_DIM)
        own_all[:, s, 1] = (top * SCORE_SCALE + jnp.log(totals)).reshape(2, rows // 2, HEAD_DIM)

    own_copy = pltpu.make_async_remote_copy(
        src_ref=own_all.at[1 - branch],
        dst_ref=own_fin.at[branch],
        send_sem=own_send,
        recv_sem=own_sem.at[0],
        device_id=(me, 1 - branch, clip),
        device_id_type=MESH,
    )
    own_copy.start()
    own_local = pltpu.make_async_copy(own_all.at[branch], own_fin.at[branch], own_sem.at[1])
    own_local.start()

    channel = (
        branch * (HALF_HEADS * HEAD_DIM)
        + lax.broadcasted_iota(jnp.int32, (HALF_HEADS, 1, HEAD_DIM), 0) * HEAD_DIM
        + lax.broadcasted_iota(jnp.int32, (HALF_HEADS, 1, HEAD_DIM), 2)
    ).astype(jnp.float32)
    frequency = jnp.exp(-math.log(1000.0) * channel / (HEADS * HEAD_DIM))
    gates = [
        1.0 + 0.5 * jnp.sin(ts_ref[s].astype(jnp.float32) * frequency) for s in range(STEPS)
    ]
    scale = 1.0 + 0.5 * gi_ref[0].astype(jnp.float32)

    def send_out(chunk, slot, code):
        pltpu.make_async_remote_copy(
            src_ref=o_buf.at[slot_rows(slot), :],
            dst_ref=o_rx.at[branch, unit_step, half_head],
            send_sem=o_send,
            recv_sem=o_sem,
            device_id=(me ^ code, half, clip),
            device_id_type=MESH,
        ).start()
        pltpu.make_async_remote_copy(
            src_ref=lse_buf.at[slot],
            dst_ref=lse_rx.at[branch, unit_step, half_head],
            send_sem=lse_send,
            recv_sem=lse_sem,
            device_id=(me ^ code, half, clip),
            device_id_type=MESH,
        ).start()

    @pl.when(has_unit)
    def _():
        pltpu.make_async_copy(kv_rx, kv_rx, kv_sem).wait()
        same_patch = (
            lax.broadcasted_iota(jnp.int32, (CHUNK, CHUNK), 0) // TOK
            == lax.broadcasted_iota(jnp.int32, (CHUNK, CHUNK), 1) // TOK
        )
        lane_token = lax.broadcasted_iota(jnp.int32, (1, TOK, HEAD_DIM), 2) % TOK
        picked = lane_token == lax.broadcasted_iota(jnp.int32, (1, TOK, HEAD_DIM), 1)
        for c in range(N_CHUNKS):
            here = pl.ds(c * CHUNK, CHUNK)
            pltpu.make_async_copy(q_rx.at[here], q_rx.at[here], q_sem.at[c]).wait()
            scores_ref[...] = lax.dot_general(
                q_rx[here, :], kv_rx[0], (((1,), (1,)), ((), ())), preferred_element_type=jnp.float32
            )
            scores_ref[:, here] = jnp.where(same_patch, MASKED, scores_ref[:, here])
            scores = scores_ref[...]
            top = jnp.max(scores, axis=1, keepdims=True)
            weights = jnp.exp2((scores - top) * (SCORE_SCALE * LOG2E)).astype(jnp.bfloat16)
            summed = jnp.dot(weights, with_ones(kv_rx[1]), preferred_element_type=jnp.float32)
            totals = summed[:, HEAD_DIM:]
            o_buf[here, :] = (summed[:, :HEAD_DIM] / totals).astype(jnp.bfloat16)
            lse = (top * SCORE_SCALE + jnp.log(totals)).reshape(CHUNK_SLOTS, TOK, HEAD_DIM)
            lse_buf[pl.ds(c * CHUNK_SLOTS, CHUNK_SLOTS)] = jnp.sum(
                jnp.where(picked, lse, 0.0), axis=1, keepdims=True
            )
            for_slots((c,), send_out)

        @pl.when(half == branch)
        def _():
            pltpu.make_async_copy(
                o_buf.at[pl.ds(SELF * TOK, TOK), :], o_rx.at[branch, unit_step, half_head], o_sem
            ).start()
            pltpu.make_async_copy(
                lse_buf.at[SELF], lse_rx.at[branch, unit_step, half_head], lse_sem
            ).start()

        @pl.when(half != branch)
        def _():
            send_out(N_CHUNKS - 1, SELF, 0)

    own_copy.wait_recv()
    own_local.wait()
    pltpu.make_async_copy(lse_rx, lse_rx, lse_sem).wait()
    pltpu.make_async_copy(o_rx, o_rx, o_sem).wait()

    token = lax.broadcasted_iota(jnp.int32, (1, TOK, HEAD_DIM), 1)
    lane = lax.broadcasted_iota(jnp.int32, (1, TOK, HEAD_DIM), 2)

    def attended(b, s):
        remote = o_rx[b, s].astype(jnp.float32)
        remote_lse = jnp.sum(jnp.where(token == lane, lse_rx[b, s], 0.0), axis=2, keepdims=True)
        own = own_fin[b, s, 0].reshape(HALF_HEADS, TOK, HEAD_DIM)
        own_lse = own_fin[b, s, 1].reshape(HALF_HEADS, TOK, HEAD_DIM)
        share = 1.0 / (1.0 + jnp.exp(own_lse - remote_lse))
        return own + share * (remote - own)

    for s in range(STEPS):
        cond = attended(0, s)
        uncond = attended(1, s)
        guided = (gates[s] * (uncond + scale * (cond - uncond))).astype(jnp.bfloat16)
        for h in range(HALF_HEADS):
            out_ref[s, :, h * HEAD_DIM : (h + 1) * HEAD_DIM] = guided[h]

    own_copy.wait_send()

    @pl.when(has_unit)
    def _():
        sent = pl.ds(0, (UNITS - 1) * TOK)
        pltpu.make_async_copy(kv_rx.at[:, sent, :], kv_rx.at[:, sent, :], kv_send).wait()
        pltpu.make_async_copy(q_rx.at[sent], q_rx.at[sent], q_send).wait()

        @pl.when(half == branch)
        def _():
            out_rows, lse_rows = pl.ds(0, SEQ_TOKENS - TOK), pl.ds(0, N_SEQ - 1)
            pltpu.make_async_copy(o_buf.at[out_rows], o_buf.at[out_rows], o_send).wait()
            pltpu.make_async_copy(lse_buf.at[lse_rows], lse_buf.at[lse_rows], lse_send).wait()

        @pl.when(half != branch)
        def _():
            pltpu.make_async_copy(o_buf, o_buf, o_send).wait()
            pltpu.make_async_copy(lse_buf, lse_buf, lse_send).wait()

    @pl.when(jnp.logical_not(has_unit))
    def _():
        sent = pl.ds(0, UNITS * TOK)
        pltpu.make_async_copy(kv_rx.at[:, sent, :], kv_rx.at[:, sent, :], kv_send).wait()
        pltpu.make_async_copy(q_rx.at[sent], q_rx.at[sent], q_send).wait()


def shards(queries, fresh_kv, stale_kv, timesteps, guidance_index):
    bf16, f32 = jnp.bfloat16, jnp.float32
    rows = HALF_HEADS * TOK
    dma = pltpu.SemaphoreType.DMA
    return pl.pallas_call(
        kernel,
        out_shape=jax.ShapeDtypeStruct((STEPS, TOK, HALF_HEADS * HEAD_DIM), bf16),
        in_specs=[pl.BlockSpec(memory_space=pltpu.HBM)] * 5,
        out_specs=pl.BlockSpec(memory_space=pltpu.VMEM),
        scratch_shapes=[
            pltpu.SMEM((STEPS,), jnp.int32),
            pltpu.SMEM((1,), jnp.int32),
            pltpu.VMEM((STEPS, TOK, HEADS * HEAD_DIM), bf16),
            pltpu.VMEM((STEPS + 1, 2, TOK, HEADS * HEAD_DIM), bf16),
            pltpu.VMEM((2, SEQ_TOKENS, HEAD_DIM), bf16),
            pltpu.VMEM((SEQ_TOKENS, HEAD_DIM), bf16),
            pltpu.VMEM((CHUNK, SEQ_TOKENS), f32),
            pltpu.VMEM((SEQ_TOKENS, HEAD_DIM), bf16),
            pltpu.VMEM((N_SEQ, 1, HEAD_DIM), f32),
            pltpu.VMEM((2, STEPS, HALF_HEADS, TOK, HEAD_DIM), bf16),
            pltpu.VMEM((2, STEPS, HALF_HEADS, 1, HEAD_DIM), f32),
            pltpu.VMEM((2, STEPS, 2, rows, HEAD_DIM), f32),
            pltpu.VMEM((2, STEPS, 2, rows, HEAD_DIM), f32),
            dma((6,)), dma, dma((N_CHUNKS,)),
            dma, dma, dma, dma,
            dma, dma, dma, dma((2,)),
        ],
        compiler_params=pltpu.CompilerParams(
            collective_id=0, has_side_effects=True, vmem_limit_bytes=60 * 2**20
        ),
        name="patch_attention",
    )(timesteps, guidance_index, queries, fresh_kv, stale_kv)


def solution(mesh):
    in_specs = (
        P(None, "cfg", ("clip", "seq"), None),
        P(None, "cfg", None, ("clip", "seq"), None),
        P("cfg", None, ("clip", "seq"), None),
        P(),
        P(),
    )
    out_specs = P(None, ("clip", "seq"), "cfg")
    return jax.shard_map(shards, mesh=mesh, in_specs=in_specs, out_specs=out_specs, check_vma=False)
```

```python
import functools
import math

import jax
import jax.numpy as jnp
from jax import lax
from jax.experimental import pallas as pl
from jax.experimental.pallas import tpu as pltpu
from jax.sharding import PartitionSpec as P

MESH = pl.DeviceIdType.MESH
HEAD_DIM = 128
HEADS = 20
HALF_HEADS = HEADS // 2
STEPS = 2
UNITS = STEPS * HEADS
TOK = 16
N_SEQ = 64
SEQ_TOKENS = TOK * N_SEQ
BRANCH_SHIFT = N_SEQ - UNITS
SCORE_SCALE = 1.0 / math.sqrt(HEAD_DIM)
LOG2E = math.log2(math.e)
MASKED = -1e30


PLANES = 4
COLUMNS = 16
FAR_PLANE = 2
NEAR_PLANES = (1, 3, 0)
CHUNK = COLUMNS * TOK


def rank_of(place):
    y, z, x = place >> 4, (place >> 2) & 3, place & 3
    return ((y ^ z) << 4) + (x << 2) + z


def holds_unit(unit):
    return jnp.logical_and(unit >= 0, unit < UNITS)


def step_and_head(unit):
    step = (unit >= HEADS).astype(jnp.int32)
    return step, unit - step * HEADS


def far_to_near(k):
    return (0x36 >> (2 * k)) & 3


def column_code(i):
    return (far_to_near(i >> 2) << 4) + far_to_near(i & 3)


def for_places(planes, body):
    def across(i, carry):
        for plane in planes:
            run = functools.partial(body, i, column_code(i) + plane * 4)
            if plane == 0:
                pl.when(i < COLUMNS - 1)(run)
            else:
                run()
        return carry

    lax.fori_loop(0, COLUMNS, across, 0)


def stacked_heads(rows):
    return jnp.concatenate(
        [rows[:, h * HEAD_DIM : (h + 1) * HEAD_DIM] for h in range(HEADS)], axis=0
    )


def with_ones(values):
    return jnp.concatenate([values, jnp.ones_like(values)], axis=1)


def kernel(
    ts_hbm, gi_hbm, q_hbm, fresh_hbm, stale_hbm, out_ref,
    ts_ref, gi_ref, q_src, kv_src, pack, rx, scores_ref, o_buf, lse_buf, o_rx, lse_rx, own_all, own_fin,
    load_sem, kv_sem, q_sem, kv_send, q_send, o_send, lse_send, o_sem, lse_sem, own_send, own_sem,
):
    me = lax.axis_index("seq")
    branch = lax.axis_index("cfg")
    clip = lax.axis_index("clip")
    my_plane = (me >> 2) & 3
    my_slot = my_plane * COLUMNS + COLUMNS - 1
    my_rank = rank_of(me)
    first_rank = BRANCH_SHIFT * branch
    unit = my_rank - first_rank
    has_unit = holds_unit(unit)
    unit_step, head = step_and_head(unit)
    half = (head >= HALF_HEADS).astype(jnp.int32)
    half_head = head - half * HALF_HEADS

    barrier = pltpu.get_barrier_semaphore()

    loads = [
        pltpu.make_async_copy(stale_hbm.at[0], kv_src.at[0], load_sem.at[0]),
        pltpu.make_async_copy(fresh_hbm.at[0, 0], kv_src.at[1], load_sem.at[1]),
        pltpu.make_async_copy(q_hbm.at[:, 0], q_src, load_sem.at[2]),
        pltpu.make_async_copy(fresh_hbm.at[1, 0], kv_src.at[2], load_sem.at[3]),
        pltpu.make_async_copy(ts_hbm, ts_ref, load_sem.at[4]),
        pltpu.make_async_copy(gi_hbm, gi_ref, load_sem.at[5]),
    ]
    for load in loads:
        load.start()

    pl.semaphore_signal(barrier, inc=1, device_id=(me, 1 - branch, clip), device_id_type=MESH)

    @pl.when(has_unit)
    def _():
        def greet(i, code):
            pl.semaphore_signal(
                barrier, inc=1, device_id=(me ^ code, branch, clip), device_id_type=MESH
            )

        for_places((FAR_PLANE,), greet)
        for_places(NEAR_PLANES, greet)

    for load in loads[:3]:
        load.wait()
    for step in range(STEPS):
        for h in range(HEADS):
            lanes = pl.ds(h * HEAD_DIM, HEAD_DIM)
            pack[step * HEADS + h, 0] = q_src[step, :, lanes]
            pack[step * HEADS + h, 1] = kv_src[step, 0, :, lanes]
            pack[step * HEADS + h, 2] = kv_src[step, 1, :, lanes]

    pl.semaphore_wait(barrier, UNITS + 1 - has_unit.astype(jnp.int32))

    def slot_rows(slot):
        return pl.ds(pl.multiple_of(slot * TOK, TOK), TOK)

    def send_kv(i, code):
        u = (my_rank ^ rank_of(code)) - first_rank

        @pl.when(holds_unit(u))
        def _():
            pltpu.make_async_remote_copy(
                src_ref=pack.at[u, pl.ds(1, 2)],
                dst_ref=rx.at[my_plane * COLUMNS + i, pl.ds(1, 2)],
                send_sem=kv_send,
                recv_sem=kv_sem,
                device_id=(me ^ code, branch, clip),
                device_id_type=MESH,
            ).start()

    def send_q(i, code):
        u = (my_rank ^ rank_of(code)) - first_rank

        @pl.when(holds_unit(u))
        def _():
            pltpu.make_async_remote_copy(
                src_ref=pack.at[u, 0],
                dst_ref=rx.at[my_plane * COLUMNS + i, 0],
                send_sem=q_send,
                recv_sem=q_sem.at[my_plane],
                device_id=(me ^ code, branch, clip),
                device_id_type=MESH,
            ).start()

    @pl.when(my_plane == 0)
    def _():
        for_places((FAR_PLANE,), send_q)
        for_places(NEAR_PLANES, send_q)

    for_places((FAR_PLANE,), send_kv)
    for_places(NEAR_PLANES, send_kv)

    @pl.when(my_plane != 0)
    def _():
        for_places((FAR_PLANE,), send_q)
        for_places(NEAR_PLANES, send_q)

    @pl.when(has_unit)
    def _():
        pltpu.make_async_copy(pack.at[unit, pl.ds(1, 2)], rx.at[my_slot, pl.ds(1, 2)], kv_sem).start()
        pltpu.make_async_copy(pack.at[unit, 0], rx.at[my_slot, 0], q_sem.at[my_plane]).start()

    for load in loads[3:]:
        load.wait()

    rows = HEADS * TOK
    same_head = (
        lax.broadcasted_iota(jnp.int32, (rows, rows), 0) // TOK
        == lax.broadcasted_iota(jnp.int32, (rows, rows), 1) // TOK
    )
    for s in range(STEPS):
        scores = lax.dot_general(
            pack[pl.ds(s * HEADS, HEADS), 0].reshape(rows, HEAD_DIM),
            stacked_heads(kv_src[s + 1, 0]),
            (((1,), (1,)), ((), ())),
            preferred_element_type=jnp.float32,
        )
        scores = jnp.where(same_head, scores, MASKED)
        top = jnp.max(scores, axis=1, keepdims=True)
        weights = jnp.exp2((scores - top) * (SCORE_SCALE * LOG2E)).astype(jnp.bfloat16)
        summed = jnp.dot(
            weights, with_ones(stacked_heads(kv_src[s + 1, 1])), preferred_element_type=jnp.float32
        )
        totals = summed[:, HEAD_DIM:]
        own_all[:, s, 0] = (summed[:, :HEAD_DIM] / totals).reshape(2, rows // 2, HEAD_DIM)
        own_all[:, s, 1] = (top * SCORE_SCALE + jnp.log(totals)).reshape(2, rows // 2, HEAD_DIM)

    own_copy = pltpu.make_async_remote_copy(
        src_ref=own_all.at[1 - branch],
        dst_ref=own_fin.at[branch],
        send_sem=own_send,
        recv_sem=own_sem.at[0],
        device_id=(me, 1 - branch, clip),
        device_id_type=MESH,
    )
    own_copy.start()
    own_local = pltpu.make_async_copy(own_all.at[branch], own_fin.at[branch], own_sem.at[1])
    own_local.start()

    channel = (
        branch * (HALF_HEADS * HEAD_DIM)
        + lax.broadcasted_iota(jnp.int32, (HALF_HEADS, 1, HEAD_DIM), 0) * HEAD_DIM
        + lax.broadcasted_iota(jnp.int32, (HALF_HEADS, 1, HEAD_DIM), 2)
    ).astype(jnp.float32)
    frequency = jnp.exp(-math.log(1000.0) * channel / (HEADS * HEAD_DIM))
    gates = [
        1.0 + 0.5 * jnp.sin(ts_ref[s].astype(jnp.float32) * frequency) for s in range(STEPS)
    ]
    scale = 1.0 + 0.5 * gi_ref[0].astype(jnp.float32)

    def send_out(slot, code):
        pltpu.make_async_remote_copy(
            src_ref=o_buf.at[slot_rows(slot), :],
            dst_ref=o_rx.at[branch, unit_step, half_head],
            send_sem=o_send,
            recv_sem=o_sem,
            device_id=(me ^ code, half, clip),
            device_id_type=MESH,
        ).start()
        pltpu.make_async_remote_copy(
            src_ref=lse_buf.at[slot],
            dst_ref=lse_rx.at[branch, unit_step, half_head],
            send_sem=lse_send,
            recv_sem=lse_sem,
            device_id=(me ^ code, half, clip),
            device_id_type=MESH,
        ).start()

    def for_chunk(c):
        away = my_plane ^ c

        def send_slot(i, carry):
            @pl.when(jnp.logical_or(away != 0, i < COLUMNS - 1))
            def _():
                send_out(c * COLUMNS + i, column_code(i) + away * 4)

            return carry

        lax.fori_loop(0, COLUMNS, send_slot, 0)

    @pl.when(has_unit)
    def _():
        kv_all = rx.at[:, pl.ds(1, 2)]
        pltpu.make_async_copy(kv_all, kv_all, kv_sem).wait()
        lane_token = lax.broadcasted_iota(jnp.int32, (1, TOK, HEAD_DIM), 2) % TOK
        picked = lane_token == lax.broadcasted_iota(jnp.int32, (1, TOK, HEAD_DIM), 1)
        same_patch = (
            lax.broadcasted_iota(jnp.int32, (CHUNK, CHUNK), 0) // TOK
            == lax.broadcasted_iota(jnp.int32, (CHUNK, CHUNK), 1) // TOK
        )
        for c in range(PLANES):
            slots, here = pl.ds(c * COLUMNS, COLUMNS), pl.ds(c * CHUNK, CHUNK)
            q_chunk = rx.at[slots, 0]
            pltpu.make_async_copy(q_chunk, q_chunk, q_sem.at[c]).wait()
            scores_ref[...] = lax.dot_general(
                q_chunk[...].reshape(CHUNK, HEAD_DIM),
                rx[:, 1].reshape(SEQ_TOKENS, HEAD_DIM),
                (((1,), (1,)), ((), ())),
                preferred_element_type=jnp.float32,
            )
            scores_ref[:, here] = jnp.where(same_patch, MASKED, scores_ref[:, here])
            scores = scores_ref[...]
            top = jnp.max(scores, axis=1, keepdims=True)
            weights = jnp.exp2((scores - top) * (SCORE_SCALE * LOG2E)).astype(jnp.bfloat16)
            summed = jnp.dot(weights, with_ones(rx[:, 2].reshape(SEQ_TOKENS, HEAD_DIM)), preferred_element_type=jnp.float32)
            totals = summed[:, HEAD_DIM:]
            o_buf[here, :] = (summed[:, :HEAD_DIM] / totals).astype(jnp.bfloat16)
            lse = (top * SCORE_SCALE + jnp.log(totals)).reshape(COLUMNS, TOK, HEAD_DIM)
            lse_buf[slots] = jnp.sum(
                jnp.where(picked, lse, 0.0), axis=1, keepdims=True
            )
            for_chunk(c)

        @pl.when(half == branch)
        def _():
            pltpu.make_async_copy(
                o_buf.at[slot_rows(my_slot), :], o_rx.at[branch, unit_step, half_head], o_sem
            ).start()
            pltpu.make_async_copy(
                lse_buf.at[my_slot], lse_rx.at[branch, unit_step, half_head], lse_sem
            ).start()

        @pl.when(half != branch)
        def _():
            send_out(my_slot, 0)

    own_copy.wait_recv()
    own_local.wait()
    pltpu.make_async_copy(lse_rx, lse_rx, lse_sem).wait()
    pltpu.make_async_copy(o_rx, o_rx, o_sem).wait()

    token = lax.broadcasted_iota(jnp.int32, (1, TOK, HEAD_DIM), 1)
    lane = lax.broadcasted_iota(jnp.int32, (1, TOK, HEAD_DIM), 2)

    def attended(b, s):
        remote = o_rx[b, s].astype(jnp.float32)
        remote_lse = jnp.sum(jnp.where(token == lane, lse_rx[b, s], 0.0), axis=2, keepdims=True)
        own = own_fin[b, s, 0].reshape(HALF_HEADS, TOK, HEAD_DIM)
        own_lse = own_fin[b, s, 1].reshape(HALF_HEADS, TOK, HEAD_DIM)
        share = 1.0 / (1.0 + jnp.exp(own_lse - remote_lse))
        return own + share * (remote - own)

    for s in range(STEPS):
        cond = attended(0, s)
        uncond = attended(1, s)
        guided = (gates[s] * (uncond + scale * (cond - uncond))).astype(jnp.bfloat16)
        for h in range(HALF_HEADS):
            out_ref[s, :, h * HEAD_DIM : (h + 1) * HEAD_DIM] = guided[h]

    def wait_sent(count):
        kv_sent, q_sent = pack.at[pl.ds(0, count), pl.ds(1, 2)], pack.at[pl.ds(0, count), 0]
        pltpu.make_async_copy(kv_sent, kv_sent, kv_send).wait()
        pltpu.make_async_copy(q_sent, q_sent, q_send).wait()

    own_copy.wait_send()

    @pl.when(has_unit)
    def _():
        wait_sent(UNITS - 1)

        @pl.when(half == branch)
        def _():
            out_rows, lse_rows = pl.ds(0, SEQ_TOKENS - TOK), pl.ds(0, N_SEQ - 1)
            pltpu.make_async_copy(o_buf.at[out_rows], o_buf.at[out_rows], o_send).wait()
            pltpu.make_async_copy(lse_buf.at[lse_rows], lse_buf.at[lse_rows], lse_send).wait()

        @pl.when(half != branch)
        def _():
            pltpu.make_async_copy(o_buf, o_buf, o_send).wait()
            pltpu.make_async_copy(lse_buf, lse_buf, lse_send).wait()

    @pl.when(jnp.logical_not(has_unit))
    def _():
        wait_sent(UNITS)


def shards(queries, fresh_kv, stale_kv, timesteps, guidance_index):
    bf16, f32 = jnp.bfloat16, jnp.float32
    rows = HALF_HEADS * TOK
    dma = pltpu.SemaphoreType.DMA
    return pl.pallas_call(
        kernel,
        out_shape=jax.ShapeDtypeStruct((STEPS, TOK, HALF_HEADS * HEAD_DIM), bf16),
        in_specs=[pl.BlockSpec(memory_space=pltpu.HBM)] * 5,
        out_specs=pl.BlockSpec(memory_space=pltpu.VMEM),
        scratch_shapes=[
            pltpu.SMEM((STEPS,), jnp.int32),
            pltpu.SMEM((1,), jnp.int32),
            pltpu.VMEM((STEPS, TOK, HEADS * HEAD_DIM), bf16),
            pltpu.VMEM((STEPS + 1, 2, TOK, HEADS * HEAD_DIM), bf16),
            pltpu.VMEM((UNITS, 3, TOK, HEAD_DIM), bf16),
            pltpu.VMEM((N_SEQ, 3, TOK, HEAD_DIM), bf16),
            pltpu.VMEM((CHUNK, SEQ_TOKENS), f32),
            pltpu.VMEM((SEQ_TOKENS, HEAD_DIM), bf16),
            pltpu.VMEM((N_SEQ, 1, HEAD_DIM), f32),
            pltpu.VMEM((2, STEPS, HALF_HEADS, TOK, HEAD_DIM), bf16),
            pltpu.VMEM((2, STEPS, HALF_HEADS, 1, HEAD_DIM), f32),
            pltpu.VMEM((2, STEPS, 2, rows, HEAD_DIM), f32),
            pltpu.VMEM((2, STEPS, 2, rows, HEAD_DIM), f32),
            dma((6,)), dma, dma((PLANES,)),
            dma, dma, dma, dma,
            dma, dma, dma, dma((2,)),
        ],
        compiler_params=pltpu.CompilerParams(
            collective_id=0, has_side_effects=True, vmem_limit_bytes=60 * 2**20
        ),
        name="patch_attention",
    )(timesteps, guidance_index, queries, fresh_kv, stale_kv)


def solution(mesh):
    in_specs = (
        P(None, "cfg", ("clip", "seq"), None),
        P(None, "cfg", None, ("clip", "seq"), None),
        P("cfg", None, ("clip", "seq"), None),
        P(),
        P(),
    )
    out_specs = P(None, ("clip", "seq"), "cfg")
    return jax.shard_map(shards, mesh=mesh, in_specs=in_specs, out_specs=out_specs, check_vma=False)
```

```python
import functools
import math

import jax
import jax.numpy as jnp
from jax import lax
from jax.experimental import pallas as pl
from jax.experimental.pallas import tpu as pltpu
from jax.sharding import PartitionSpec as P

MESH = pl.DeviceIdType.MESH
HEAD_DIM = 128
HEADS = 20
HALF_HEADS = HEADS // 2
STEPS = 2
UNITS = STEPS * HEADS
TOK = 16
N_SEQ = 64
SEQ_TOKENS = TOK * N_SEQ
EARLY_UNITS = 12
LATE_UNITS = UNITS // 2 - EARLY_UNITS
RELEASE_ORDER = (0xF8635210 - 2**32, 0xFFF7FF94 - 2**32)
SCORE_SCALE = 1.0 / math.sqrt(HEAD_DIM)
LOG2E = math.log2(math.e)
MASKED = -1e30


PLANES = 4
COLUMNS = 16
FAR_PLANE = 2
NEAR_PLANES = (1, 3, 0)
CHUNK = COLUMNS * TOK


def unit_of(place, branch):
    y, z, x = place >> 4, (place >> 2) & 3, place & 3
    order = jnp.where(y >= 2, RELEASE_ORDER[1], RELEASE_ORDER[0])
    late_rank = (order >> (((y & 1) << 4) + (x << 2))) & 15
    early_rank = (((y ^ z) << 2) + x) ^ (15 * branch)
    late = z >= 2
    rank = jnp.where(late, late_rank, early_rank)
    first = jnp.where(late, 2 * EARLY_UNITS + (z - 2) * LATE_UNITS, z * EARLY_UNITS)
    return first + rank, rank < jnp.where(late, LATE_UNITS, EARLY_UNITS)


def step_and_head(unit):
    step = (unit >= HEADS).astype(jnp.int32)
    return step, unit - step * HEADS


def far_to_near(k):
    return (0x36 >> (2 * k)) & 3


def column_code(i):
    return (far_to_near(i >> 2) << 4) + far_to_near(i & 3)


def for_places(planes, body):
    def across(i, carry):
        for plane in planes:
            run = functools.partial(body, i, column_code(i) + plane * 4)
            if plane == 0:
                pl.when(i < COLUMNS - 1)(run)
            else:
                run()
        return carry

    lax.fori_loop(0, COLUMNS, across, 0)


def stacked_heads(rows):
    return jnp.concatenate(
        [rows[:, h * HEAD_DIM : (h + 1) * HEAD_DIM] for h in range(HEADS)], axis=0
    )


def with_ones(values):
    return jnp.concatenate([values, jnp.ones_like(values)], axis=1)


def kernel(
    ts_hbm, gi_hbm, q_hbm, fresh_hbm, stale_hbm, out_ref,
    ts_ref, gi_ref, q_src, kv_src, pack, rx, scores_ref, o_buf, lse_buf, o_rx, lse_rx, own_all, own_fin,
    load_sem, kv_sem, q_sem, kv_send, q_send, o_send, lse_send, o_sem, lse_sem, own_send, own_sem,
):
    me = lax.axis_index("seq")
    branch = lax.axis_index("cfg")
    clip = lax.axis_index("clip")
    my_plane = (me >> 2) & 3
    my_slot = my_plane * COLUMNS + COLUMNS - 1
    unit, has_unit = unit_of(me, branch)
    unit_step, head = step_and_head(unit)
    half = (head >= HALF_HEADS).astype(jnp.int32)
    half_head = head - half * HALF_HEADS

    barrier = pltpu.get_barrier_semaphore()

    loads = [
        pltpu.make_async_copy(stale_hbm.at[0], kv_src.at[0], load_sem.at[0]),
        pltpu.make_async_copy(fresh_hbm.at[0, 0], kv_src.at[1], load_sem.at[1]),
        pltpu.make_async_copy(q_hbm.at[:, 0], q_src, load_sem.at[2]),
        pltpu.make_async_copy(fresh_hbm.at[1, 0], kv_src.at[2], load_sem.at[3]),
        pltpu.make_async_copy(ts_hbm, ts_ref, load_sem.at[4]),
        pltpu.make_async_copy(gi_hbm, gi_ref, load_sem.at[5]),
    ]
    for load in loads:
        load.start()

    pl.semaphore_signal(barrier, inc=1, device_id=(me, 1 - branch, clip), device_id_type=MESH)

    @pl.when(has_unit)
    def _():
        def greet(i, code):
            pl.semaphore_signal(
                barrier, inc=1, device_id=(me ^ code, branch, clip), device_id_type=MESH
            )

        for_places((FAR_PLANE,), greet)
        for_places(NEAR_PLANES, greet)

    for load in loads[:3]:
        load.wait()
    for step in range(STEPS):
        for h in range(HEADS):
            lanes = pl.ds(h * HEAD_DIM, HEAD_DIM)
            pack[step * HEADS + h, 0] = q_src[step, :, lanes]
            pack[step * HEADS + h, 1] = kv_src[step, 0, :, lanes]
            pack[step * HEADS + h, 2] = kv_src[step, 1, :, lanes]

    pl.semaphore_wait(barrier, UNITS + 1 - has_unit.astype(jnp.int32))

    def slot_rows(slot):
        return pl.ds(pl.multiple_of(slot * TOK, TOK), TOK)

    def send_kv(i, code):
        u, held = unit_of(me ^ code, branch)

        @pl.when(held)
        def _():
            pltpu.make_async_remote_copy(
                src_ref=pack.at[u, pl.ds(1, 2)],
                dst_ref=rx.at[my_plane * COLUMNS + i, pl.ds(1, 2)],
                send_sem=kv_send,
                recv_sem=kv_sem,
                device_id=(me ^ code, branch, clip),
                device_id_type=MESH,
            ).start()

    def send_q(i, code):
        u, held = unit_of(me ^ code, branch)

        @pl.when(held)
        def _():
            pltpu.make_async_remote_copy(
                src_ref=pack.at[u, 0],
                dst_ref=rx.at[my_plane * COLUMNS + i, 0],
                send_sem=q_send,
                recv_sem=q_sem.at[my_plane],
                device_id=(me ^ code, branch, clip),
                device_id_type=MESH,
            ).start()

    @pl.when(my_plane == 0)
    def _():
        for_places((FAR_PLANE,), send_q)
        for_places(NEAR_PLANES, send_q)

    for_places((FAR_PLANE,), send_kv)
    for_places(NEAR_PLANES, send_kv)

    @pl.when(my_plane != 0)
    def _():
        for_places((FAR_PLANE,), send_q)
        for_places(NEAR_PLANES, send_q)

    @pl.when(has_unit)
    def _():
        pltpu.make_async_copy(pack.at[unit, pl.ds(1, 2)], rx.at[my_slot, pl.ds(1, 2)], kv_sem).start()
        pltpu.make_async_copy(pack.at[unit, 0], rx.at[my_slot, 0], q_sem.at[my_plane]).start()

    for load in loads[3:]:
        load.wait()

    rows = HEADS * TOK
    same_head = (
        lax.broadcasted_iota(jnp.int32, (rows, rows), 0) // TOK
        == lax.broadcasted_iota(jnp.int32, (rows, rows), 1) // TOK
    )
    for s in range(STEPS):
        scores = lax.dot_general(
            pack[pl.ds(s * HEADS, HEADS), 0].reshape(rows, HEAD_DIM),
            stacked_heads(kv_src[s + 1, 0]),
            (((1,), (1,)), ((), ())),
            preferred_element_type=jnp.float32,
        )
        scores = jnp.where(same_head, scores, MASKED)
        top = jnp.max(scores, axis=1, keepdims=True)
        weights = jnp.exp2((scores - top) * (SCORE_SCALE * LOG2E)).astype(jnp.bfloat16)
        summed = jnp.dot(
            weights, with_ones(stacked_heads(kv_src[s + 1, 1])), preferred_element_type=jnp.float32
        )
        totals = summed[:, HEAD_DIM:]
        own_all[:, s, 0] = (summed[:, :HEAD_DIM] / totals).reshape(2, rows // 2, HEAD_DIM)
        own_all[:, s, 1] = (top * SCORE_SCALE + jnp.log(totals)).reshape(2, rows // 2, HEAD_DIM)

    own_copy = pltpu.make_async_remote_copy(
        src_ref=own_all.at[1 - branch],
        dst_ref=own_fin.at[branch],
        send_sem=own_send,
        recv_sem=own_sem.at[0],
        device_id=(me, 1 - branch, clip),
        device_id_type=MESH,
    )
    own_copy.start()
    own_local = pltpu.make_async_copy(own_all.at[branch], own_fin.at[branch], own_sem.at[1])
    own_local.start()

    channel = (
        branch * (HALF_HEADS * HEAD_DIM)
        + lax.broadcasted_iota(jnp.int32, (HALF_HEADS, 1, HEAD_DIM), 0) * HEAD_DIM
        + lax.broadcasted_iota(jnp.int32, (HALF_HEADS, 1, HEAD_DIM), 2)
    ).astype(jnp.float32)
    frequency = jnp.exp(-math.log(1000.0) * channel / (HEADS * HEAD_DIM))
    gates = [
        1.0 + 0.5 * jnp.sin(ts_ref[s].astype(jnp.float32) * frequency) for s in range(STEPS)
    ]
    scale = 1.0 + 0.5 * gi_ref[0].astype(jnp.float32)

    def send_out(slot, code):
        pltpu.make_async_remote_copy(
            src_ref=o_buf.at[slot_rows(slot), :],
            dst_ref=o_rx.at[branch, unit_step, half_head],
            send_sem=o_send,
            recv_sem=o_sem,
            device_id=(me ^ code, half, clip),
            device_id_type=MESH,
        ).start()
        pltpu.make_async_remote_copy(
            src_ref=lse_buf.at[slot],
            dst_ref=lse_rx.at[branch, unit_step, half_head],
            send_sem=lse_send,
            recv_sem=lse_sem,
            device_id=(me ^ code, half, clip),
            device_id_type=MESH,
        ).start()

    def for_chunk(c):
        away = my_plane ^ c

        def send_slot(i, carry):
            @pl.when(jnp.logical_or(away != 0, i < COLUMNS - 1))
            def _():
                send_out(c * COLUMNS + i, column_code(i) + away * 4)

            return carry

        lax.fori_loop(0, COLUMNS, send_slot, 0)

    @pl.when(has_unit)
    def _():
        kv_all = rx.at[:, pl.ds(1, 2)]
        pltpu.make_async_copy(kv_all, kv_all, kv_sem).wait()
        lane_token = lax.broadcasted_iota(jnp.int32, (1, TOK, HEAD_DIM), 2) % TOK
        picked = lane_token == lax.broadcasted_iota(jnp.int32, (1, TOK, HEAD_DIM), 1)
        same_patch = (
            lax.broadcasted_iota(jnp.int32, (CHUNK, CHUNK), 0) // TOK
            == lax.broadcasted_iota(jnp.int32, (CHUNK, CHUNK), 1) // TOK
        )
        for c in range(PLANES):
            slots, here = pl.ds(c * COLUMNS, COLUMNS), pl.ds(c * CHUNK, CHUNK)
            q_chunk = rx.at[slots, 0]
            pltpu.make_async_copy(q_chunk, q_chunk, q_sem.at[c]).wait()
            scores_ref[...] = lax.dot_general(
                q_chunk[...].reshape(CHUNK, HEAD_DIM),
                rx[:, 1].reshape(SEQ_TOKENS, HEAD_DIM),
                (((1,), (1,)), ((), ())),
                preferred_element_type=jnp.float32,
            )
            scores_ref[:, here] = jnp.where(same_patch, MASKED, scores_ref[:, here])
            scores = scores_ref[...]
            top = jnp.max(scores, axis=1, keepdims=True)
            weights = jnp.exp2((scores - top) * (SCORE_SCALE * LOG2E)).astype(jnp.bfloat16)
            summed = jnp.dot(weights, with_ones(rx[:, 2].reshape(SEQ_TOKENS, HEAD_DIM)), preferred_element_type=jnp.float32)
            totals = summed[:, HEAD_DIM:]
            o_buf[here, :] = (summed[:, :HEAD_DIM] / totals).astype(jnp.bfloat16)
            lse = (top * SCORE_SCALE + jnp.log(totals)).reshape(COLUMNS, TOK, HEAD_DIM)
            lse_buf[slots] = jnp.sum(
                jnp.where(picked, lse, 0.0), axis=1, keepdims=True
            )
            for_chunk(c)

        @pl.when(half == branch)
        def _():
            pltpu.make_async_copy(
                o_buf.at[slot_rows(my_slot), :], o_rx.at[branch, unit_step, half_head], o_sem
            ).start()
            pltpu.make_async_copy(
                lse_buf.at[my_slot], lse_rx.at[branch, unit_step, half_head], lse_sem
            ).start()

        @pl.when(half != branch)
        def _():
            send_out(my_slot, 0)

    own_copy.wait_recv()
    own_local.wait()
    pltpu.make_async_copy(lse_rx, lse_rx, lse_sem).wait()
    pltpu.make_async_copy(o_rx, o_rx, o_sem).wait()

    token = lax.broadcasted_iota(jnp.int32, (1, TOK, HEAD_DIM), 1)
    lane = lax.broadcasted_iota(jnp.int32, (1, TOK, HEAD_DIM), 2)

    def attended(b, s):
        remote = o_rx[b, s].astype(jnp.float32)
        remote_lse = jnp.sum(jnp.where(token == lane, lse_rx[b, s], 0.0), axis=2, keepdims=True)
        own = own_fin[b, s, 0].reshape(HALF_HEADS, TOK, HEAD_DIM)
        own_lse = own_fin[b, s, 1].reshape(HALF_HEADS, TOK, HEAD_DIM)
        share = 1.0 / (1.0 + jnp.exp(own_lse - remote_lse))
        return own + share * (remote - own)

    for s in range(STEPS):
        cond = attended(0, s)
        uncond = attended(1, s)
        guided = (gates[s] * (uncond + scale * (cond - uncond))).astype(jnp.bfloat16)
        for h in range(HALF_HEADS):
            out_ref[s, :, h * HEAD_DIM : (h + 1) * HEAD_DIM] = guided[h]

    def wait_sent(count):
        kv_sent, q_sent = pack.at[pl.ds(0, count), pl.ds(1, 2)], pack.at[pl.ds(0, count), 0]
        pltpu.make_async_copy(kv_sent, kv_sent, kv_send).wait()
        pltpu.make_async_copy(q_sent, q_sent, q_send).wait()

    own_copy.wait_send()

    @pl.when(has_unit)
    def _():
        wait_sent(UNITS - 1)

        @pl.when(half == branch)
        def _():
            out_rows, lse_rows = pl.ds(0, SEQ_TOKENS - TOK), pl.ds(0, N_SEQ - 1)
            pltpu.make_async_copy(o_buf.at[out_rows], o_buf.at[out_rows], o_send).wait()
            pltpu.make_async_copy(lse_buf.at[lse_rows], lse_buf.at[lse_rows], lse_send).wait()

        @pl.when(half != branch)
        def _():
            pltpu.make_async_copy(o_buf, o_buf, o_send).wait()
            pltpu.make_async_copy(lse_buf, lse_buf, lse_send).wait()

    @pl.when(jnp.logical_not(has_unit))
    def _():
        wait_sent(UNITS)


def shards(queries, fresh_kv, stale_kv, timesteps, guidance_index):
    bf16, f32 = jnp.bfloat16, jnp.float32
    rows = HALF_HEADS * TOK
    dma = pltpu.SemaphoreType.DMA
    return pl.pallas_call(
        kernel,
        out_shape=jax.ShapeDtypeStruct((STEPS, TOK, HALF_HEADS * HEAD_DIM), bf16),
        in_specs=[pl.BlockSpec(memory_space=pltpu.HBM)] * 5,
        out_specs=pl.BlockSpec(memory_space=pltpu.VMEM),
        scratch_shapes=[
            pltpu.SMEM((STEPS,), jnp.int32),
            pltpu.SMEM((1,), jnp.int32),
            pltpu.VMEM((STEPS, TOK, HEADS * HEAD_DIM), bf16),
            pltpu.VMEM((STEPS + 1, 2, TOK, HEADS * HEAD_DIM), bf16),
            pltpu.VMEM((UNITS, 3, TOK, HEAD_DIM), bf16),
            pltpu.VMEM((N_SEQ, 3, TOK, HEAD_DIM), bf16),
            pltpu.VMEM((CHUNK, SEQ_TOKENS), f32),
            pltpu.VMEM((SEQ_TOKENS, HEAD_DIM), bf16),
            pltpu.VMEM((N_SEQ, 1, HEAD_DIM), f32),
            pltpu.VMEM((2, STEPS, HALF_HEADS, TOK, HEAD_DIM), bf16),
            pltpu.VMEM((2, STEPS, HALF_HEADS, 1, HEAD_DIM), f32),
            pltpu.VMEM((2, STEPS, 2, rows, HEAD_DIM), f32),
            pltpu.VMEM((2, STEPS, 2, rows, HEAD_DIM), f32),
            dma((6,)), dma, dma((PLANES,)),
            dma, dma, dma, dma,
            dma, dma, dma, dma((2,)),
        ],
        compiler_params=pltpu.CompilerParams(
            collective_id=0, has_side_effects=True, vmem_limit_bytes=60 * 2**20
        ),
        name="patch_attention",
    )(timesteps, guidance_index, queries, fresh_kv, stale_kv)


def solution(mesh):
    in_specs = (
        P(None, "cfg", ("clip", "seq"), None),
        P(None, "cfg", None, ("clip", "seq"), None),
        P("cfg", None, ("clip", "seq"), None),
        P(),
        P(),
    )
    out_specs = P(None, ("clip", "seq"), "cfg")
    return jax.shard_map(shards, mesh=mesh, in_specs=in_specs, out_specs=out_specs, check_vma=False)
```

```python
import functools
import math

import jax
import jax.numpy as jnp
from jax import lax
from jax.experimental import pallas as pl
from jax.experimental.pallas import tpu as pltpu
from jax.sharding import PartitionSpec as P

MESH = pl.DeviceIdType.MESH
HEAD_DIM = 128
HEADS = 20
HALF_HEADS = HEADS // 2
STEPS = 2
UNITS = STEPS * HEADS
TOK = 16
N_SEQ = 64
SEQ_TOKENS = TOK * N_SEQ
EARLY_UNITS = 12
LATE_UNITS = UNITS // 2 - EARLY_UNITS
RELEASE_ORDER = (0xF8635210 - 2**32, 0xFFF7FF94 - 2**32)
SCORE_SCALE = 1.0 / math.sqrt(HEAD_DIM)
LOG2E = math.log2(math.e)
MASKED = -1e30
VMEM_GRANT = 538 * 2**20 // 10


PLANES = 4
COLUMNS = 16
FAR_PLANE = 2
NEAR_PLANES = (1, 3, 0)
CHUNK = COLUMNS * TOK


def unit_of(place, branch):
    y, z, x = place >> 4, (place >> 2) & 3, place & 3
    order = jnp.where(y >= 2, RELEASE_ORDER[1], RELEASE_ORDER[0])
    late_rank = (order >> (((y & 1) << 4) + (x << 2))) & 15
    early_rank = (((y ^ z) << 2) + x) ^ (15 * branch)
    late = z >= 2
    rank = jnp.where(late, late_rank, early_rank)
    first = jnp.where(late, 2 * EARLY_UNITS + (z - 2) * LATE_UNITS, z * EARLY_UNITS)
    return first + rank, rank < jnp.where(late, LATE_UNITS, EARLY_UNITS)


def step_and_head(unit):
    step = (unit >= HEADS).astype(jnp.int32)
    return step, unit - step * HEADS


def far_to_near(k):
    return (0x36 >> (2 * k)) & 3


def column_code(i):
    return (far_to_near(i >> 2) << 4) + far_to_near(i & 3)


def for_places(planes, body):
    def across(i, carry):
        for plane in planes:
            run = functools.partial(body, i, column_code(i) + plane * 4)
            if plane == 0:
                pl.when(i < COLUMNS - 1)(run)
            else:
                run()
        return carry

    lax.fori_loop(0, COLUMNS, across, 0)


def stacked_heads(rows):
    return jnp.concatenate(
        [rows[:, h * HEAD_DIM : (h + 1) * HEAD_DIM] for h in range(HEADS)], axis=0
    )


def with_ones(values):
    return jnp.concatenate([values, jnp.ones_like(values)], axis=1)


def kernel(
    ts_hbm, gi_hbm, q_hbm, fresh_hbm, stale_hbm, out_ref,
    ts_ref, gi_ref, q_src, kv_src, pack, rx, scores_ref, o_buf, lse_buf, o_rx, lse_rx, own_all, own_fin,
    load_sem, kv_sem, q_sem, kv_send, q_send, o_send, lse_send, o_sem, lse_sem, own_send, own_sem,
):
    me = lax.axis_index("seq")
    branch = lax.axis_index("cfg")
    clip = lax.axis_index("clip")
    my_plane = (me >> 2) & 3
    my_slot = my_plane * COLUMNS + COLUMNS - 1
    unit, has_unit = unit_of(me, branch)
    unit_step, head = step_and_head(unit)
    half = (head >= HALF_HEADS).astype(jnp.int32)
    half_head = head - half * HALF_HEADS

    barrier = pltpu.get_barrier_semaphore()

    loads = [
        pltpu.make_async_copy(stale_hbm.at[0], kv_src.at[0], load_sem.at[0]),
        pltpu.make_async_copy(fresh_hbm.at[0, 0], kv_src.at[1], load_sem.at[1]),
        pltpu.make_async_copy(q_hbm.at[:, 0], q_src, load_sem.at[2]),
        pltpu.make_async_copy(fresh_hbm.at[1, 0], kv_src.at[2], load_sem.at[3]),
        pltpu.make_async_copy(ts_hbm, ts_ref, load_sem.at[4]),
        pltpu.make_async_copy(gi_hbm, gi_ref, load_sem.at[5]),
    ]
    for load in loads:
        load.start()

    pl.semaphore_signal(barrier, inc=1, device_id=(me, 1 - branch, clip), device_id_type=MESH)

    @pl.when(has_unit)
    def _():
        def greet(i, code):
            pl.semaphore_signal(
                barrier, inc=1, device_id=(me ^ code, branch, clip), device_id_type=MESH
            )

        for_places((FAR_PLANE,), greet)
        for_places(NEAR_PLANES, greet)

    for load in loads[:3]:
        load.wait()
    for step in range(STEPS):
        for h in range(HEADS):
            lanes = pl.ds(h * HEAD_DIM, HEAD_DIM)
            pack[step * HEADS + h, 0] = q_src[step, :, lanes]
            pack[step * HEADS + h, 1] = kv_src[step, 0, :, lanes]
            pack[step * HEADS + h, 2] = kv_src[step, 1, :, lanes]

    pl.semaphore_wait(barrier, UNITS + 1 - has_unit.astype(jnp.int32))

    def slot_rows(slot):
        return pl.ds(pl.multiple_of(slot * TOK, TOK), TOK)

    def send_kv(i, code):
        u, held = unit_of(me ^ code, branch)

        @pl.when(held)
        def _():
            pltpu.make_async_remote_copy(
                src_ref=pack.at[u, pl.ds(1, 2)],
                dst_ref=rx.at[my_plane * COLUMNS + i, pl.ds(1, 2)],
                send_sem=kv_send,
                recv_sem=kv_sem,
                device_id=(me ^ code, branch, clip),
                device_id_type=MESH,
            ).start()

    def send_q(i, code):
        u, held = unit_of(me ^ code, branch)

        @pl.when(held)
        def _():
            pltpu.make_async_remote_copy(
                src_ref=pack.at[u, 0],
                dst_ref=rx.at[my_plane * COLUMNS + i, 0],
                send_sem=q_send,
                recv_sem=q_sem.at[my_plane],
                device_id=(me ^ code, branch, clip),
                device_id_type=MESH,
            ).start()

    @pl.when(my_plane == 0)
    def _():
        for_places((FAR_PLANE,), send_q)
        for_places(NEAR_PLANES, send_q)

    for_places((FAR_PLANE,), send_kv)
    for_places(NEAR_PLANES, send_kv)

    @pl.when(my_plane != 0)
    def _():
        for_places((FAR_PLANE,), send_q)
        for_places(NEAR_PLANES, send_q)

    @pl.when(has_unit)
    def _():
        pltpu.make_async_copy(pack.at[unit, pl.ds(1, 2)], rx.at[my_slot, pl.ds(1, 2)], kv_sem).start()
        pltpu.make_async_copy(pack.at[unit, 0], rx.at[my_slot, 0], q_sem.at[my_plane]).start()

    for load in loads[3:]:
        load.wait()

    rows = HEADS * TOK
    same_head = (
        lax.broadcasted_iota(jnp.int32, (rows, rows), 0) // TOK
        == lax.broadcasted_iota(jnp.int32, (rows, rows), 1) // TOK
    )
    for s in range(STEPS):
        scores = lax.dot_general(
            pack[pl.ds(s * HEADS, HEADS), 0].reshape(rows, HEAD_DIM),
            stacked_heads(kv_src[s + 1, 0]),
            (((1,), (1,)), ((), ())),
            preferred_element_type=jnp.float32,
        )
        scores = jnp.where(same_head, scores, MASKED)
        top = jnp.max(scores, axis=1, keepdims=True)
        weights = jnp.exp2((scores - top) * (SCORE_SCALE * LOG2E)).astype(jnp.bfloat16)
        summed = jnp.dot(
            weights, with_ones(stacked_heads(kv_src[s + 1, 1])), preferred_element_type=jnp.float32
        )
        totals = summed[:, HEAD_DIM:]
        own_all[:, s, 0] = (summed[:, :HEAD_DIM] / totals).reshape(2, rows // 2, HEAD_DIM)
        own_all[:, s, 1] = (top * SCORE_SCALE + jnp.log(totals)).reshape(2, rows // 2, HEAD_DIM)

    own_copy = pltpu.make_async_remote_copy(
        src_ref=own_all.at[1 - branch],
        dst_ref=own_fin.at[branch],
        send_sem=own_send,
        recv_sem=own_sem.at[0],
        device_id=(me, 1 - branch, clip),
        device_id_type=MESH,
    )
    own_copy.start()
    own_local = pltpu.make_async_copy(own_all.at[branch], own_fin.at[branch], own_sem.at[1])
    own_local.start()

    channel = (
        branch * (HALF_HEADS * HEAD_DIM)
        + lax.broadcasted_iota(jnp.int32, (HALF_HEADS, 1, HEAD_DIM), 0) * HEAD_DIM
        + lax.broadcasted_iota(jnp.int32, (HALF_HEADS, 1, HEAD_DIM), 2)
    ).astype(jnp.float32)
    frequency = jnp.exp(-math.log(1000.0) * channel / (HEADS * HEAD_DIM))
    gates = [
        1.0 + 0.5 * jnp.sin(ts_ref[s].astype(jnp.float32) * frequency) for s in range(STEPS)
    ]
    scale = 1.0 + 0.5 * gi_ref[0].astype(jnp.float32)

    def send_out(slot, code):
        pltpu.make_async_remote_copy(
            src_ref=o_buf.at[slot_rows(slot), :],
            dst_ref=o_rx.at[branch, unit_step, half_head],
            send_sem=o_send,
            recv_sem=o_sem,
            device_id=(me ^ code, half, clip),
            device_id_type=MESH,
        ).start()
        pltpu.make_async_remote_copy(
            src_ref=lse_buf.at[slot],
            dst_ref=lse_rx.at[branch, unit_step, half_head],
            send_sem=lse_send,
            recv_sem=lse_sem,
            device_id=(me ^ code, half, clip),
            device_id_type=MESH,
        ).start()

    def for_chunk(c):
        away = my_plane ^ c

        def send_slot(i, carry):
            @pl.when(jnp.logical_or(away != 0, i < COLUMNS - 1))
            def _():
                send_out(c * COLUMNS + i, column_code(i) + away * 4)

            return carry

        lax.fori_loop(0, COLUMNS, send_slot, 0)

    @pl.when(has_unit)
    def _():
        kv_all = rx.at[:, pl.ds(1, 2)]
        pltpu.make_async_copy(kv_all, kv_all, kv_sem).wait()
        lane_token = lax.broadcasted_iota(jnp.int32, (1, TOK, HEAD_DIM), 2) % TOK
        picked = lane_token == lax.broadcasted_iota(jnp.int32, (1, TOK, HEAD_DIM), 1)
        same_patch = (
            lax.broadcasted_iota(jnp.int32, (CHUNK, CHUNK), 0) // TOK
            == lax.broadcasted_iota(jnp.int32, (CHUNK, CHUNK), 1) // TOK
        )
        for c in range(PLANES):
            slots, here = pl.ds(c * COLUMNS, COLUMNS), pl.ds(c * CHUNK, CHUNK)
            q_chunk = rx.at[slots, 0]
            pltpu.make_async_copy(q_chunk, q_chunk, q_sem.at[c]).wait()
            scores_ref[...] = lax.dot_general(
                q_chunk[...].reshape(CHUNK, HEAD_DIM),
                rx[:, 1].reshape(SEQ_TOKENS, HEAD_DIM),
                (((1,), (1,)), ((), ())),
                preferred_element_type=jnp.float32,
            )
            scores_ref[:, here] = jnp.where(same_patch, MASKED, scores_ref[:, here])
            scores = scores_ref[...]
            top = jnp.max(scores, axis=1, keepdims=True)
            weights = jnp.exp2((scores - top) * (SCORE_SCALE * LOG2E)).astype(jnp.bfloat16)
            summed = jnp.dot(weights, with_ones(rx[:, 2].reshape(SEQ_TOKENS, HEAD_DIM)), preferred_element_type=jnp.float32)
            totals = summed[:, HEAD_DIM:]
            o_buf[here, :] = (summed[:, :HEAD_DIM] / totals).astype(jnp.bfloat16)
            lse = (top * SCORE_SCALE + jnp.log(totals)).reshape(COLUMNS, TOK, HEAD_DIM)
            lse_buf[slots] = jnp.sum(
                jnp.where(picked, lse, 0.0), axis=1, keepdims=True
            )
            for_chunk(c)

        @pl.when(half == branch)
        def _():
            pltpu.make_async_copy(
                o_buf.at[slot_rows(my_slot), :], o_rx.at[branch, unit_step, half_head], o_sem
            ).start()
            pltpu.make_async_copy(
                lse_buf.at[my_slot], lse_rx.at[branch, unit_step, half_head], lse_sem
            ).start()

        @pl.when(half != branch)
        def _():
            send_out(my_slot, 0)

    own_copy.wait_recv()
    own_local.wait()
    pltpu.make_async_copy(lse_rx, lse_rx, lse_sem).wait()
    pltpu.make_async_copy(o_rx, o_rx, o_sem).wait()

    token = lax.broadcasted_iota(jnp.int32, (1, TOK, HEAD_DIM), 1)
    lane = lax.broadcasted_iota(jnp.int32, (1, TOK, HEAD_DIM), 2)

    def attended(b, s):
        remote = o_rx[b, s].astype(jnp.float32)
        remote_lse = jnp.sum(jnp.where(token == lane, lse_rx[b, s], 0.0), axis=2, keepdims=True)
        own = own_fin[b, s, 0].reshape(HALF_HEADS, TOK, HEAD_DIM)
        own_lse = own_fin[b, s, 1].reshape(HALF_HEADS, TOK, HEAD_DIM)
        share = 1.0 / (1.0 + jnp.exp(own_lse - remote_lse))
        return own + share * (remote - own)

    for s in range(STEPS):
        cond = attended(0, s)
        uncond = attended(1, s)
        guided = (gates[s] * (uncond + scale * (cond - uncond))).astype(jnp.bfloat16)
        for h in range(HALF_HEADS):
            out_ref[s, :, h * HEAD_DIM : (h + 1) * HEAD_DIM] = guided[h]

    def wait_sent(count):
        kv_sent, q_sent = pack.at[pl.ds(0, count), pl.ds(1, 2)], pack.at[pl.ds(0, count), 0]
        pltpu.make_async_copy(kv_sent, kv_sent, kv_send).wait()
        pltpu.make_async_copy(q_sent, q_sent, q_send).wait()

    own_copy.wait_send()

    @pl.when(has_unit)
    def _():
        wait_sent(UNITS - 1)

        @pl.when(half == branch)
        def _():
            out_rows, lse_rows = pl.ds(0, SEQ_TOKENS - TOK), pl.ds(0, N_SEQ - 1)
            pltpu.make_async_copy(o_buf.at[out_rows], o_buf.at[out_rows], o_send).wait()
            pltpu.make_async_copy(lse_buf.at[lse_rows], lse_buf.at[lse_rows], lse_send).wait()

        @pl.when(half != branch)
        def _():
            pltpu.make_async_copy(o_buf, o_buf, o_send).wait()
            pltpu.make_async_copy(lse_buf, lse_buf, lse_send).wait()

    @pl.when(jnp.logical_not(has_unit))
    def _():
        wait_sent(UNITS)


def shards(queries, fresh_kv, stale_kv, timesteps, guidance_index):
    bf16, f32 = jnp.bfloat16, jnp.float32
    rows = HALF_HEADS * TOK
    dma = pltpu.SemaphoreType.DMA
    return pl.pallas_call(
        kernel,
        out_shape=jax.ShapeDtypeStruct((STEPS, TOK, HALF_HEADS * HEAD_DIM), bf16),
        in_specs=[pl.BlockSpec(memory_space=pltpu.HBM)] * 5,
        out_specs=pl.BlockSpec(memory_space=pltpu.VMEM),
        scratch_shapes=[
            pltpu.SMEM((STEPS,), jnp.int32),
            pltpu.SMEM((1,), jnp.int32),
            pltpu.VMEM((STEPS, TOK, HEADS * HEAD_DIM), bf16),
            pltpu.VMEM((STEPS + 1, 2, TOK, HEADS * HEAD_DIM), bf16),
            pltpu.VMEM((UNITS, 3, TOK, HEAD_DIM), bf16),
            pltpu.VMEM((N_SEQ, 3, TOK, HEAD_DIM), bf16),
            pltpu.VMEM((CHUNK, SEQ_TOKENS), f32),
            pltpu.VMEM((SEQ_TOKENS, HEAD_DIM), bf16),
            pltpu.VMEM((N_SEQ, 1, HEAD_DIM), f32),
            pltpu.VMEM((2, STEPS, HALF_HEADS, TOK, HEAD_DIM), bf16),
            pltpu.VMEM((2, STEPS, HALF_HEADS, 1, HEAD_DIM), f32),
            pltpu.VMEM((2, STEPS, 2, rows, HEAD_DIM), f32),
            pltpu.VMEM((2, STEPS, 2, rows, HEAD_DIM), f32),
            dma((6,)), dma, dma((PLANES,)),
            dma, dma, dma, dma,
            dma, dma, dma, dma((2,)),
        ],
        compiler_params=pltpu.CompilerParams(
            collective_id=0, has_side_effects=True, vmem_limit_bytes=VMEM_GRANT
        ),
        name="patch_attention",
    )(timesteps, guidance_index, queries, fresh_kv, stale_kv)


def solution(mesh):
    in_specs = (
        P(None, "cfg", ("clip", "seq"), None),
        P(None, "cfg", None, ("clip", "seq"), None),
        P("cfg", None, ("clip", "seq"), None),
        P(),
        P(),
    )
    out_specs = P(None, ("clip", "seq"), "cfg")
    return jax.shard_map(shards, mesh=mesh, in_specs=in_specs, out_specs=out_specs, check_vma=False)
```

```python
import functools
import math

import jax
import jax.numpy as jnp
from jax import lax
from jax.experimental import pallas as pl
from jax.experimental.pallas import tpu as pltpu
from jax.sharding import PartitionSpec as P

MESH = pl.DeviceIdType.MESH
HEAD_DIM = 128
HEADS = 20
HALF_HEADS = HEADS // 2
STEPS = 2
UNITS = STEPS * HEADS
TOK = 16
N_SEQ = 64
SEQ_TOKENS = TOK * N_SEQ
EARLY_UNITS = 12
LATE_UNITS = UNITS // 2 - EARLY_UNITS
RELEASE_ORDER = (0xF8635210 - 2**32, 0xFFF7FF94 - 2**32)
SCORE_SCALE = 1.0 / math.sqrt(HEAD_DIM)
LOG2E = math.log2(math.e)
MASKED = -1e30
VMEM_GRANT = 538 * 2**20 // 10


PLANES = 4
COLUMNS = 16
FAR_PLANE = 2
NEAR_PLANES = (1, 3, 0)
CHUNK = COLUMNS * TOK


def unit_of(place, branch):
    y, z, x = place >> 4, (place >> 2) & 3, place & 3
    order = jnp.where(y >= 2, RELEASE_ORDER[1], RELEASE_ORDER[0])
    late_rank = (order >> (((y & 1) << 4) + (x << 2))) & 15
    early_rank = (((y ^ z) << 2) + x) ^ (15 * branch)
    late = z >= 2
    rank = jnp.where(late, late_rank, early_rank)
    first = jnp.where(late, 2 * EARLY_UNITS + (z - 2) * LATE_UNITS, z * EARLY_UNITS)
    return first + rank, rank < jnp.where(late, LATE_UNITS, EARLY_UNITS)


def step_and_head(unit):
    step = (unit >= HEADS).astype(jnp.int32)
    return step, unit - step * HEADS


def far_to_near(k):
    return (0x36 >> (2 * k)) & 3


def column_code(i):
    return (far_to_near(i >> 2) << 4) + far_to_near(i & 3)


def for_places(planes, body):
    def across(i, carry):
        for plane in planes:
            run = functools.partial(body, i, column_code(i) + plane * 4)
            if plane == 0:
                pl.when(i < COLUMNS - 1)(run)
            else:
                run()
        return carry

    lax.fori_loop(0, COLUMNS, across, 0)


def stacked_heads(rows):
    return jnp.concatenate(
        [rows[:, h * HEAD_DIM : (h + 1) * HEAD_DIM] for h in range(HEADS)], axis=0
    )


def with_ones(values):
    return jnp.concatenate([values, jnp.ones_like(values)], axis=1)


def kernel(
    ts_hbm, gi_hbm, q_hbm, fresh_hbm, stale_hbm, out_ref,
    ts_ref, gi_ref, q_src, kv_src, pack, rx, scores_ref, o_buf, lse_buf, o_rx, lse_rx, own_all, own_fin,
    load_sem, kv_sem, q_sem, kv_send, q_send, o_send, lse_send, o_sem, lse_sem, own_send, own_sem,
):
    me = lax.axis_index("seq")
    branch = lax.axis_index("cfg")
    clip = lax.axis_index("clip")
    my_plane = (me >> 2) & 3
    my_slot = my_plane * COLUMNS + COLUMNS - 1
    unit, has_unit = unit_of(me, branch)
    unit_step, head = step_and_head(unit)
    half = (head >= HALF_HEADS).astype(jnp.int32)
    half_head = head - half * HALF_HEADS

    barrier = pltpu.get_barrier_semaphore()

    loads = [
        pltpu.make_async_copy(stale_hbm.at[0], kv_src.at[0], load_sem.at[0]),
        pltpu.make_async_copy(fresh_hbm.at[0, 0], kv_src.at[1], load_sem.at[1]),
        pltpu.make_async_copy(q_hbm.at[:, 0], q_src, load_sem.at[2]),
        pltpu.make_async_copy(fresh_hbm.at[1, 0], kv_src.at[2], load_sem.at[3]),
        pltpu.make_async_copy(ts_hbm, ts_ref, load_sem.at[4]),
        pltpu.make_async_copy(gi_hbm, gi_ref, load_sem.at[5]),
    ]
    pl.semaphore_signal(barrier, inc=1, device_id=(me, 1 - branch, clip), device_id_type=MESH)

    @pl.when(has_unit)
    def _():
        def greet(i, code):
            pl.semaphore_signal(
                barrier, inc=1, device_id=(me ^ code, branch, clip), device_id_type=MESH
            )

        for_places((FAR_PLANE,), greet)
        for_places(NEAR_PLANES, greet)

    for load in loads:
        load.start()

    for load in loads[:3]:
        load.wait()
    for step in range(STEPS):
        for h in range(HEADS):
            lanes = pl.ds(h * HEAD_DIM, HEAD_DIM)
            pack[step * HEADS + h, 0] = q_src[step, :, lanes]
            pack[step * HEADS + h, 1] = kv_src[step, 0, :, lanes]
            pack[step * HEADS + h, 2] = kv_src[step, 1, :, lanes]

    pl.semaphore_wait(barrier, UNITS + 1 - has_unit.astype(jnp.int32))

    def slot_rows(slot):
        return pl.ds(pl.multiple_of(slot * TOK, TOK), TOK)

    def send_kv(i, code):
        u, held = unit_of(me ^ code, branch)

        @pl.when(held)
        def _():
            pltpu.make_async_remote_copy(
                src_ref=pack.at[u, pl.ds(1, 2)],
                dst_ref=rx.at[my_plane * COLUMNS + i, pl.ds(1, 2)],
                send_sem=kv_send,
                recv_sem=kv_sem,
                device_id=(me ^ code, branch, clip),
                device_id_type=MESH,
            ).start()

    def send_q(i, code):
        u, held = unit_of(me ^ code, branch)

        @pl.when(held)
        def _():
            pltpu.make_async_remote_copy(
                src_ref=pack.at[u, 0],
                dst_ref=rx.at[my_plane * COLUMNS + i, 0],
                send_sem=q_send,
                recv_sem=q_sem.at[my_plane],
                device_id=(me ^ code, branch, clip),
                device_id_type=MESH,
            ).start()

    @pl.when(my_plane == 0)
    def _():
        for_places((FAR_PLANE,), send_q)
        for_places(NEAR_PLANES, send_q)

    for_places((FAR_PLANE,), send_kv)
    for_places(NEAR_PLANES, send_kv)

    @pl.when(my_plane != 0)
    def _():
        for_places((FAR_PLANE,), send_q)
        for_places(NEAR_PLANES, send_q)

    @pl.when(has_unit)
    def _():
        pltpu.make_async_copy(pack.at[unit, pl.ds(1, 2)], rx.at[my_slot, pl.ds(1, 2)], kv_sem).start()
        pltpu.make_async_copy(pack.at[unit, 0], rx.at[my_slot, 0], q_sem.at[my_plane]).start()

    for load in loads[3:]:
        load.wait()

    rows = HEADS * TOK
    same_head = (
        lax.broadcasted_iota(jnp.int32, (rows, rows), 0) // TOK
        == lax.broadcasted_iota(jnp.int32, (rows, rows), 1) // TOK
    )
    for s in range(STEPS):
        scores = lax.dot_general(
            pack[pl.ds(s * HEADS, HEADS), 0].reshape(rows, HEAD_DIM),
            stacked_heads(kv_src[s + 1, 0]),
            (((1,), (1,)), ((), ())),
            preferred_element_type=jnp.float32,
        )
        scores = jnp.where(same_head, scores, MASKED)
        top = jnp.max(scores, axis=1, keepdims=True)
        weights = jnp.exp2((scores - top) * (SCORE_SCALE * LOG2E)).astype(jnp.bfloat16)
        summed = jnp.dot(
            weights, with_ones(stacked_heads(kv_src[s + 1, 1])), preferred_element_type=jnp.float32
        )
        totals = summed[:, HEAD_DIM:]
        own_all[:, s, 0] = (summed[:, :HEAD_DIM] / totals).reshape(2, rows // 2, HEAD_DIM)
        own_all[:, s, 1] = (top * SCORE_SCALE + jnp.log(totals)).reshape(2, rows // 2, HEAD_DIM)

    own_copy = pltpu.make_async_remote_copy(
        src_ref=own_all.at[1 - branch],
        dst_ref=own_fin.at[branch],
        send_sem=own_send,
        recv_sem=own_sem.at[0],
        device_id=(me, 1 - branch, clip),
        device_id_type=MESH,
    )
    own_copy.start()
    own_local = pltpu.make_async_copy(own_all.at[branch], own_fin.at[branch], own_sem.at[1])
    own_local.start()

    channel = (
        branch * (HALF_HEADS * HEAD_DIM)
        + lax.broadcasted_iota(jnp.int32, (HALF_HEADS, 1, HEAD_DIM), 0) * HEAD_DIM
        + lax.broadcasted_iota(jnp.int32, (HALF_HEADS, 1, HEAD_DIM), 2)
    ).astype(jnp.float32)
    frequency = jnp.exp(-math.log(1000.0) * channel / (HEADS * HEAD_DIM))
    gates = [
        1.0 + 0.5 * jnp.sin(ts_ref[s].astype(jnp.float32) * frequency) for s in range(STEPS)
    ]
    scale = 1.0 + 0.5 * gi_ref[0].astype(jnp.float32)

    def send_out(slot, code):
        pltpu.make_async_remote_copy(
            src_ref=o_buf.at[slot_rows(slot), :],
            dst_ref=o_rx.at[branch, unit_step, half_head],
            send_sem=o_send,
            recv_sem=o_sem,
            device_id=(me ^ code, half, clip),
            device_id_type=MESH,
        ).start()
        pltpu.make_async_remote_copy(
            src_ref=lse_buf.at[slot],
            dst_ref=lse_rx.at[branch, unit_step, half_head],
            send_sem=lse_send,
            recv_sem=lse_sem,
            device_id=(me ^ code, half, clip),
            device_id_type=MESH,
        ).start()

    def for_chunk(c):
        away = my_plane ^ c

        def send_slots(k, carry):
            for m in range(3):
                i = 3 * k + m
                send_out(c * COLUMNS + i, column_code(i) + away * 4)
            return carry

        lax.fori_loop(0, (COLUMNS - 1) // 3, send_slots, 0)

        @pl.when(away != 0)
        def _():
            send_out(c * COLUMNS + COLUMNS - 1, away * 4)

    @pl.when(has_unit)
    def _():
        kv_all = rx.at[:, pl.ds(1, 2)]
        pltpu.make_async_copy(kv_all, kv_all, kv_sem).wait()
        lane_token = lax.broadcasted_iota(jnp.int32, (1, TOK, HEAD_DIM), 2) % TOK
        picked = lane_token == lax.broadcasted_iota(jnp.int32, (1, TOK, HEAD_DIM), 1)
        same_patch = (
            lax.broadcasted_iota(jnp.int32, (CHUNK, CHUNK), 0) // TOK
            == lax.broadcasted_iota(jnp.int32, (CHUNK, CHUNK), 1) // TOK
        )
        for c in range(PLANES):
            slots, here = pl.ds(c * COLUMNS, COLUMNS), pl.ds(c * CHUNK, CHUNK)
            q_chunk = rx.at[slots, 0]
            pltpu.make_async_copy(q_chunk, q_chunk, q_sem.at[c]).wait()
            scores_ref[...] = lax.dot_general(
                q_chunk[...].reshape(CHUNK, HEAD_DIM),
                rx[:, 1].reshape(SEQ_TOKENS, HEAD_DIM),
                (((1,), (1,)), ((), ())),
                preferred_element_type=jnp.float32,
            )
            scores_ref[:, here] = jnp.where(same_patch, MASKED, scores_ref[:, here])
            scores = scores_ref[...]
            top = jnp.max(scores, axis=1, keepdims=True)
            weights = jnp.exp2((scores - top) * (SCORE_SCALE * LOG2E)).astype(jnp.bfloat16)
            summed = jnp.dot(weights, with_ones(rx[:, 2].reshape(SEQ_TOKENS, HEAD_DIM)), preferred_element_type=jnp.float32)
            totals = summed[:, HEAD_DIM:]
            o_buf[here, :] = (summed[:, :HEAD_DIM] / totals).astype(jnp.bfloat16)
            lse = (top * SCORE_SCALE + jnp.log(totals)).reshape(COLUMNS, TOK, HEAD_DIM)
            lse_buf[slots] = jnp.sum(
                jnp.where(picked, lse, 0.0), axis=1, keepdims=True
            )
            for_chunk(c)

        @pl.when(half == branch)
        def _():
            pltpu.make_async_copy(
                o_buf.at[slot_rows(my_slot), :], o_rx.at[branch, unit_step, half_head], o_sem
            ).start()
            pltpu.make_async_copy(
                lse_buf.at[my_slot], lse_rx.at[branch, unit_step, half_head], lse_sem
            ).start()

        @pl.when(half != branch)
        def _():
            send_out(my_slot, 0)

    own_copy.wait_recv()
    own_local.wait()
    pltpu.make_async_copy(lse_rx, lse_rx, lse_sem).wait()
    pltpu.make_async_copy(o_rx, o_rx, o_sem).wait()

    token = lax.broadcasted_iota(jnp.int32, (1, TOK, HEAD_DIM), 1)
    lane = lax.broadcasted_iota(jnp.int32, (1, TOK, HEAD_DIM), 2)

    def attended(b, s):
        remote = o_rx[b, s].astype(jnp.float32)
        remote_lse = jnp.sum(jnp.where(token == lane, lse_rx[b, s], 0.0), axis=2, keepdims=True)
        own = own_fin[b, s, 0].reshape(HALF_HEADS, TOK, HEAD_DIM)
        own_lse = own_fin[b, s, 1].reshape(HALF_HEADS, TOK, HEAD_DIM)
        share = 1.0 / (1.0 + jnp.exp(own_lse - remote_lse))
        return own + share * (remote - own)

    for s in range(STEPS):
        cond = attended(0, s)
        uncond = attended(1, s)
        guided = (gates[s] * (uncond + scale * (cond - uncond))).astype(jnp.bfloat16)
        for h in range(HALF_HEADS):
            out_ref[s, :, h * HEAD_DIM : (h + 1) * HEAD_DIM] = guided[h]

    def wait_sent(count):
        kv_sent, q_sent = pack.at[pl.ds(0, count), pl.ds(1, 2)], pack.at[pl.ds(0, count), 0]
        pltpu.make_async_copy(kv_sent, kv_sent, kv_send).wait()
        pltpu.make_async_copy(q_sent, q_sent, q_send).wait()

    own_copy.wait_send()

    @pl.when(has_unit)
    def _():
        wait_sent(UNITS - 1)

        @pl.when(half == branch)
        def _():
            out_rows, lse_rows = pl.ds(0, SEQ_TOKENS - TOK), pl.ds(0, N_SEQ - 1)
            pltpu.make_async_copy(o_buf.at[out_rows], o_buf.at[out_rows], o_send).wait()
            pltpu.make_async_copy(lse_buf.at[lse_rows], lse_buf.at[lse_rows], lse_send).wait()

        @pl.when(half != branch)
        def _():
            pltpu.make_async_copy(o_buf, o_buf, o_send).wait()
            pltpu.make_async_copy(lse_buf, lse_buf, lse_send).wait()

    @pl.when(jnp.logical_not(has_unit))
    def _():
        wait_sent(UNITS)


def shards(queries, fresh_kv, stale_kv, timesteps, guidance_index):
    bf16, f32 = jnp.bfloat16, jnp.float32
    rows = HALF_HEADS * TOK
    dma = pltpu.SemaphoreType.DMA
    return pl.pallas_call(
        kernel,
        out_shape=jax.ShapeDtypeStruct((STEPS, TOK, HALF_HEADS * HEAD_DIM), bf16),
        in_specs=[pl.BlockSpec(memory_space=pltpu.HBM)] * 5,
        out_specs=pl.BlockSpec(memory_space=pltpu.VMEM),
        scratch_shapes=[
            pltpu.SMEM((STEPS,), jnp.int32),
            pltpu.SMEM((1,), jnp.int32),
            pltpu.VMEM((STEPS, TOK, HEADS * HEAD_DIM), bf16),
            pltpu.VMEM((STEPS + 1, 2, TOK, HEADS * HEAD_DIM), bf16),
            pltpu.VMEM((UNITS, 3, TOK, HEAD_DIM), bf16),
            pltpu.VMEM((N_SEQ, 3, TOK, HEAD_DIM), bf16),
            pltpu.VMEM((CHUNK, SEQ_TOKENS), f32),
            pltpu.VMEM((SEQ_TOKENS, HEAD_DIM), bf16),
            pltpu.VMEM((N_SEQ, 1, HEAD_DIM), f32),
            pltpu.VMEM((2, STEPS, HALF_HEADS, TOK, HEAD_DIM), bf16),
            pltpu.VMEM((2, STEPS, HALF_HEADS, 1, HEAD_DIM), f32),
            pltpu.VMEM((2, STEPS, 2, rows, HEAD_DIM), f32),
            pltpu.VMEM((2, STEPS, 2, rows, HEAD_DIM), f32),
            dma((6,)), dma, dma((PLANES,)),
            dma, dma, dma, dma,
            dma, dma, dma, dma((2,)),
        ],
        compiler_params=pltpu.CompilerParams(
            collective_id=0, has_side_effects=True, vmem_limit_bytes=VMEM_GRANT
        ),
        name="patch_attention",
    )(timesteps, guidance_index, queries, fresh_kv, stale_kv)


def solution(mesh):
    in_specs = (
        P(None, "cfg", ("clip", "seq"), None),
        P(None, "cfg", None, ("clip", "seq"), None),
        P("cfg", None, ("clip", "seq"), None),
        P(),
        P(),
    )
    out_specs = P(None, ("clip", "seq"), "cfg")
    return jax.shard_map(shards, mesh=mesh, in_specs=in_specs, out_specs=out_specs, check_vma=False)
```

```python
import functools
import math

import jax
import jax.numpy as jnp
from jax import lax
from jax.experimental import pallas as pl
from jax.experimental.pallas import tpu as pltpu
from jax.sharding import PartitionSpec as P

MESH = pl.DeviceIdType.MESH
HEAD_DIM = 128
HEADS = 20
HALF_HEADS = HEADS // 2
STEPS = 2
UNITS = STEPS * HEADS
TOK = 16
N_SEQ = 64
SEQ_TOKENS = TOK * N_SEQ
EARLY_UNITS = 12
LATE_UNITS = UNITS // 2 - EARLY_UNITS
RELEASE_ORDER = (0xF8635210 - 2**32, 0xFFF7FF94 - 2**32)
SCORE_SCALE = 1.0 / math.sqrt(HEAD_DIM)
LOG2E = math.log2(math.e)
MASKED = -1e30
VMEM_GRANT = 538 * 2**20 // 10


PLANES = 4
COLUMNS = 16
FAR_PLANE = 2
NEAR_PLANES = (1, 3, 0)
CHUNK = COLUMNS * TOK


def unit_of(place, branch):
    y, z, x = place >> 4, (place >> 2) & 3, place & 3
    order = jnp.where(y >= 2, RELEASE_ORDER[1], RELEASE_ORDER[0])
    late_rank = (order >> (((y & 1) << 4) + (x << 2))) & 15
    early_rank = (((y ^ z) << 2) + x) ^ (15 * branch)
    late = z >= 2
    rank = jnp.where(late, late_rank, early_rank)
    first = jnp.where(late, 2 * EARLY_UNITS + (z - 2) * LATE_UNITS, z * EARLY_UNITS)
    return first + rank, rank < jnp.where(late, LATE_UNITS, EARLY_UNITS)


def step_and_head(unit):
    step = (unit >= HEADS).astype(jnp.int32)
    return step, unit - step * HEADS


def far_to_near(k):
    return (0x36 >> (2 * k)) & 3


def column_code(i):
    return (far_to_near(i >> 2) << 4) + far_to_near(i & 3)


def for_places(planes, body):
    def across(i, carry):
        for plane in planes:
            run = functools.partial(body, i, column_code(i) + plane * 4)
            if plane == 0:
                pl.when(i < COLUMNS - 1)(run)
            else:
                run()
        return carry

    lax.fori_loop(0, COLUMNS, across, 0)


def stacked_heads(rows):
    return jnp.concatenate(
        [rows[:, h * HEAD_DIM : (h + 1) * HEAD_DIM] for h in range(HEADS)], axis=0
    )


def with_ones(values):
    return jnp.concatenate([values, jnp.ones_like(values)], axis=1)


def kernel(
    ts_hbm, gi_hbm, q_hbm, fresh_hbm, stale_hbm, out_ref,
    ts_ref, gi_ref, q_src, kv_src, pack, rx, scores_ref, o_buf, lse_buf, o_rx, lse_rx, own_all, own_fin,
    load_sem, kv_sem, q_sem, kv_send, q_send, o_send, lse_send, o_sem, lse_sem, own_send, own_sem,
):
    me = lax.axis_index("seq")
    branch = lax.axis_index("cfg")
    clip = lax.axis_index("clip")
    my_plane = (me >> 2) & 3
    my_slot = my_plane * COLUMNS + COLUMNS - 1
    unit, has_unit = unit_of(me, branch)
    unit_step, head = step_and_head(unit)
    half = (head >= HALF_HEADS).astype(jnp.int32)
    half_head = head - half * HALF_HEADS

    barrier = pltpu.get_barrier_semaphore()

    loads = [
        pltpu.make_async_copy(stale_hbm.at[0], kv_src.at[0], load_sem.at[0]),
        pltpu.make_async_copy(fresh_hbm.at[0, 0], kv_src.at[1], load_sem.at[1]),
        pltpu.make_async_copy(q_hbm.at[:, 0], q_src, load_sem.at[2]),
        pltpu.make_async_copy(fresh_hbm.at[1, 0], kv_src.at[2], load_sem.at[3]),
        pltpu.make_async_copy(ts_hbm, ts_ref, load_sem.at[4]),
        pltpu.make_async_copy(gi_hbm, gi_ref, load_sem.at[5]),
    ]
    pl.semaphore_signal(barrier, inc=1, device_id=(me, 1 - branch, clip), device_id_type=MESH)

    @pl.when(has_unit)
    def _():
        def greet(i, code):
            pl.semaphore_signal(
                barrier, inc=1, device_id=(me ^ code, branch, clip), device_id_type=MESH
            )

        for_places((FAR_PLANE,), greet)
        for_places(NEAR_PLANES, greet)

    for load in loads:
        load.start()

    for load in loads[:3]:
        load.wait()
    for step in range(STEPS):
        for h in range(HEADS):
            lanes = pl.ds(h * HEAD_DIM, HEAD_DIM)
            pack[step * HEADS + h, 0] = q_src[step, :, lanes]
            pack[step * HEADS + h, 1] = kv_src[step, 0, :, lanes]
            pack[step * HEADS + h, 2] = kv_src[step, 1, :, lanes]

    pl.semaphore_wait(barrier, UNITS + 1 - has_unit.astype(jnp.int32))

    def slot_rows(slot):
        return pl.ds(pl.multiple_of(slot * TOK, TOK), TOK)

    def send_kv(i, code):
        u, held = unit_of(me ^ code, branch)

        @pl.when(held)
        def _():
            pltpu.make_async_remote_copy(
                src_ref=pack.at[u, pl.ds(1, 2)],
                dst_ref=rx.at[my_plane * COLUMNS + i, pl.ds(1, 2)],
                send_sem=kv_send,
                recv_sem=kv_sem,
                device_id=(me ^ code, branch, clip),
                device_id_type=MESH,
            ).start()

    def send_q(i, code):
        u, held = unit_of(me ^ code, branch)

        @pl.when(held)
        def _():
            pltpu.make_async_remote_copy(
                src_ref=pack.at[u, 0],
                dst_ref=rx.at[my_plane * COLUMNS + i, 0],
                send_sem=q_send,
                recv_sem=q_sem.at[my_plane],
                device_id=(me ^ code, branch, clip),
                device_id_type=MESH,
            ).start()

    @pl.when(my_plane == 0)
    def _():
        for_places((FAR_PLANE,), send_q)
        for_places(NEAR_PLANES, send_q)

    for_places((FAR_PLANE,), send_kv)
    for_places(NEAR_PLANES, send_kv)

    @pl.when(my_plane != 0)
    def _():
        for_places((FAR_PLANE,), send_q)
        for_places(NEAR_PLANES, send_q)

    @pl.when(has_unit)
    def _():
        pltpu.make_async_copy(pack.at[unit, pl.ds(1, 2)], rx.at[my_slot, pl.ds(1, 2)], kv_sem).start()
        pltpu.make_async_copy(pack.at[unit, 0], rx.at[my_slot, 0], q_sem.at[my_plane]).start()

    for load in loads[3:]:
        load.wait()

    rows = HEADS * TOK
    same_head = (
        lax.broadcasted_iota(jnp.int32, (rows, rows), 0) // TOK
        == lax.broadcasted_iota(jnp.int32, (rows, rows), 1) // TOK
    )
    for s in range(STEPS):
        scores = lax.dot_general(
            pack[pl.ds(s * HEADS, HEADS), 0].reshape(rows, HEAD_DIM),
            stacked_heads(kv_src[s + 1, 0]),
            (((1,), (1,)), ((), ())),
            preferred_element_type=jnp.float32,
        )
        scores = jnp.where(same_head, scores, MASKED)
        top = jnp.max(scores, axis=1, keepdims=True)
        weights = jnp.exp2((scores - top) * (SCORE_SCALE * LOG2E)).astype(jnp.bfloat16)
        summed = jnp.dot(
            weights, with_ones(stacked_heads(kv_src[s + 1, 1])), preferred_element_type=jnp.float32
        )
        totals = summed[:, HEAD_DIM:]
        own_all[:, s, 0] = (summed[:, :HEAD_DIM] / totals).reshape(2, rows // 2, HEAD_DIM)
        own_all[:, s, 1] = (top * SCORE_SCALE + jnp.log(totals)).reshape(2, rows // 2, HEAD_DIM)

    own_copy = pltpu.make_async_remote_copy(
        src_ref=own_all.at[1 - branch],
        dst_ref=own_fin.at[branch],
        send_sem=own_send,
        recv_sem=own_sem.at[0],
        device_id=(me, 1 - branch, clip),
        device_id_type=MESH,
    )
    own_copy.start()
    own_local = pltpu.make_async_copy(own_all.at[branch], own_fin.at[branch], own_sem.at[1])
    own_local.start()

    channel = (
        branch * (HALF_HEADS * HEAD_DIM)
        + lax.broadcasted_iota(jnp.int32, (HALF_HEADS, 1, HEAD_DIM), 0) * HEAD_DIM
        + lax.broadcasted_iota(jnp.int32, (HALF_HEADS, 1, HEAD_DIM), 2)
    ).astype(jnp.float32)
    frequency = jnp.exp(-math.log(1000.0) * channel / (HEADS * HEAD_DIM))
    gates = [
        1.0 + 0.5 * jnp.sin(ts_ref[s].astype(jnp.float32) * frequency) for s in range(STEPS)
    ]
    scale = 1.0 + 0.5 * gi_ref[0].astype(jnp.float32)

    def send_out(slot, code):
        pltpu.make_async_remote_copy(
            src_ref=o_buf.at[slot_rows(slot), :],
            dst_ref=o_rx.at[branch, unit_step, half_head],
            send_sem=o_send,
            recv_sem=o_sem.at[unit_step],
            device_id=(me ^ code, half, clip),
            device_id_type=MESH,
        ).start()
        pltpu.make_async_remote_copy(
            src_ref=lse_buf.at[slot],
            dst_ref=lse_rx.at[branch, unit_step, half_head],
            send_sem=lse_send,
            recv_sem=lse_sem.at[unit_step],
            device_id=(me ^ code, half, clip),
            device_id_type=MESH,
        ).start()

    def for_chunk(c):
        away = my_plane ^ c

        def send_slots(k, carry):
            for m in range(3):
                i = 3 * k + m
                send_out(c * COLUMNS + i, column_code(i) + away * 4)
            return carry

        lax.fori_loop(0, (COLUMNS - 1) // 3, send_slots, 0)

        @pl.when(away != 0)
        def _():
            send_out(c * COLUMNS + COLUMNS - 1, away * 4)

    @pl.when(has_unit)
    def _():
        kv_all = rx.at[:, pl.ds(1, 2)]
        pltpu.make_async_copy(kv_all, kv_all, kv_sem).wait()
        lane_token = lax.broadcasted_iota(jnp.int32, (1, TOK, HEAD_DIM), 2) % TOK
        picked = lane_token == lax.broadcasted_iota(jnp.int32, (1, TOK, HEAD_DIM), 1)
        same_patch = (
            lax.broadcasted_iota(jnp.int32, (CHUNK, CHUNK), 0) // TOK
            == lax.broadcasted_iota(jnp.int32, (CHUNK, CHUNK), 1) // TOK
        )
        for c in range(PLANES):
            slots, here = pl.ds(c * COLUMNS, COLUMNS), pl.ds(c * CHUNK, CHUNK)
            q_chunk = rx.at[slots, 0]
            pltpu.make_async_copy(q_chunk, q_chunk, q_sem.at[c]).wait()
            scores_ref[...] = lax.dot_general(
                q_chunk[...].reshape(CHUNK, HEAD_DIM),
                rx[:, 1].reshape(SEQ_TOKENS, HEAD_DIM),
                (((1,), (1,)), ((), ())),
                preferred_element_type=jnp.float32,
            )
            scores_ref[:, here] = jnp.where(same_patch, MASKED, scores_ref[:, here])
            scores = scores_ref[...]
            top = jnp.max(scores, axis=1, keepdims=True)
            weights = jnp.exp2((scores - top) * (SCORE_SCALE * LOG2E)).astype(jnp.bfloat16)
            summed = jnp.dot(weights, with_ones(rx[:, 2].reshape(SEQ_TOKENS, HEAD_DIM)), preferred_element_type=jnp.float32)
            totals = summed[:, HEAD_DIM:]
            o_buf[here, :] = (summed[:, :HEAD_DIM] / totals).astype(jnp.bfloat16)
            lse = (top * SCORE_SCALE + jnp.log(totals)).reshape(COLUMNS, TOK, HEAD_DIM)
            lse_buf[slots] = jnp.sum(
                jnp.where(picked, lse, 0.0), axis=1, keepdims=True
            )
            for_chunk(c)

        @pl.when(half == branch)
        def _():
            pltpu.make_async_copy(
                o_buf.at[slot_rows(my_slot), :], o_rx.at[branch, unit_step, half_head], o_sem.at[unit_step]
            ).start()
            pltpu.make_async_copy(
                lse_buf.at[my_slot], lse_rx.at[branch, unit_step, half_head], lse_sem.at[unit_step]
            ).start()

        @pl.when(half != branch)
        def _():
            send_out(my_slot, 0)

    own_copy.wait_recv()
    own_local.wait()

    token = lax.broadcasted_iota(jnp.int32, (1, TOK, HEAD_DIM), 1)
    lane = lax.broadcasted_iota(jnp.int32, (1, TOK, HEAD_DIM), 2)

    def attended(b, s):
        remote = o_rx[b, s].astype(jnp.float32)
        remote_lse = jnp.sum(jnp.where(token == lane, lse_rx[b, s], 0.0), axis=2, keepdims=True)
        own = own_fin[b, s, 0].reshape(HALF_HEADS, TOK, HEAD_DIM)
        own_lse = own_fin[b, s, 1].reshape(HALF_HEADS, TOK, HEAD_DIM)
        share = 1.0 / (1.0 + jnp.exp(own_lse - remote_lse))
        return own + share * (remote - own)

    for s in range(STEPS):
        pltpu.make_async_copy(lse_rx.at[:, s], lse_rx.at[:, s], lse_sem.at[s]).wait()
        pltpu.make_async_copy(o_rx.at[:, s], o_rx.at[:, s], o_sem.at[s]).wait()
        cond = attended(0, s)
        uncond = attended(1, s)
        guided = (gates[s] * (uncond + scale * (cond - uncond))).astype(jnp.bfloat16)
        for h in range(HALF_HEADS):
            out_ref[s, :, h * HEAD_DIM : (h + 1) * HEAD_DIM] = guided[h]

    def wait_sent(count):
        kv_sent, q_sent = pack.at[pl.ds(0, count), pl.ds(1, 2)], pack.at[pl.ds(0, count), 0]
        pltpu.make_async_copy(kv_sent, kv_sent, kv_send).wait()
        pltpu.make_async_copy(q_sent, q_sent, q_send).wait()

    own_copy.wait_send()

    @pl.when(has_unit)
    def _():
        wait_sent(UNITS - 1)

        @pl.when(half == branch)
        def _():
            out_rows, lse_rows = pl.ds(0, SEQ_TOKENS - TOK), pl.ds(0, N_SEQ - 1)
            pltpu.make_async_copy(o_buf.at[out_rows], o_buf.at[out_rows], o_send).wait()
            pltpu.make_async_copy(lse_buf.at[lse_rows], lse_buf.at[lse_rows], lse_send).wait()

        @pl.when(half != branch)
        def _():
            pltpu.make_async_copy(o_buf, o_buf, o_send).wait()
            pltpu.make_async_copy(lse_buf, lse_buf, lse_send).wait()

    @pl.when(jnp.logical_not(has_unit))
    def _():
        wait_sent(UNITS)


def shards(queries, fresh_kv, stale_kv, timesteps, guidance_index):
    bf16, f32 = jnp.bfloat16, jnp.float32
    rows = HALF_HEADS * TOK
    dma = pltpu.SemaphoreType.DMA
    return pl.pallas_call(
        kernel,
        out_shape=jax.ShapeDtypeStruct((STEPS, TOK, HALF_HEADS * HEAD_DIM), bf16),
        in_specs=[pl.BlockSpec(memory_space=pltpu.HBM)] * 5,
        out_specs=pl.BlockSpec(memory_space=pltpu.VMEM),
        scratch_shapes=[
            pltpu.SMEM((STEPS,), jnp.int32),
            pltpu.SMEM((1,), jnp.int32),
            pltpu.VMEM((STEPS, TOK, HEADS * HEAD_DIM), bf16),
            pltpu.VMEM((STEPS + 1, 2, TOK, HEADS * HEAD_DIM), bf16),
            pltpu.VMEM((UNITS, 3, TOK, HEAD_DIM), bf16),
            pltpu.VMEM((N_SEQ, 3, TOK, HEAD_DIM), bf16),
            pltpu.VMEM((CHUNK, SEQ_TOKENS), f32),
            pltpu.VMEM((SEQ_TOKENS, HEAD_DIM), bf16),
            pltpu.VMEM((N_SEQ, 1, HEAD_DIM), f32),
            pltpu.VMEM((2, STEPS, HALF_HEADS, TOK, HEAD_DIM), bf16),
            pltpu.VMEM((2, STEPS, HALF_HEADS, 1, HEAD_DIM), f32),
            pltpu.VMEM((2, STEPS, 2, rows, HEAD_DIM), f32),
            pltpu.VMEM((2, STEPS, 2, rows, HEAD_DIM), f32),
            dma((6,)), dma, dma((PLANES,)),
            dma, dma, dma, dma,
            dma((STEPS,)), dma((STEPS,)), dma, dma((2,)),
        ],
        compiler_params=pltpu.CompilerParams(
            collective_id=0, has_side_effects=True, vmem_limit_bytes=VMEM_GRANT
        ),
        name="patch_attention",
    )(timesteps, guidance_index, queries, fresh_kv, stale_kv)


def solution(mesh):
    in_specs = (
        P(None, "cfg", ("clip", "seq"), None),
        P(None, "cfg", None, ("clip", "seq"), None),
        P("cfg", None, ("clip", "seq"), None),
        P(),
        P(),
    )
    out_specs = P(None, ("clip", "seq"), "cfg")
    return jax.shard_map(shards, mesh=mesh, in_specs=in_specs, out_specs=out_specs, check_vma=False)
```

```python
import functools
import math

import jax
import jax.numpy as jnp
from jax import lax
from jax.experimental import pallas as pl
from jax.experimental.pallas import tpu as pltpu
from jax.sharding import PartitionSpec as P

MESH = pl.DeviceIdType.MESH
HEAD_DIM = 128
HEADS = 20
HALF_HEADS = HEADS // 2
STEPS = 2
UNITS = STEPS * HEADS
TOK = 16
N_SEQ = 64
SEQ_TOKENS = TOK * N_SEQ
EARLY_UNITS = 12
LATE_UNITS = UNITS // 2 - EARLY_UNITS
RELEASE_ORDER = (0xF8635210 - 2**32, 0xFFF7FF94 - 2**32)
SCORE_SCALE = 1.0 / math.sqrt(HEAD_DIM)
LOG2E = math.log2(math.e)
MASKED = -1e30
VMEM_GRANT = 538 * 2**20 // 10


PLANES = 4
COLUMNS = 16
FAR_PLANE = 2
NEAR_PLANES = (1, 3, 0)
CHUNK = COLUMNS * TOK


def unit_of(place, branch):
    y, z, x = place >> 4, (place >> 2) & 3, place & 3
    order = jnp.where(y >= 2, RELEASE_ORDER[1], RELEASE_ORDER[0])
    late_rank = (order >> (((y & 1) << 4) + (x << 2))) & 15
    early_rank = (((y ^ z) << 2) + x) ^ (15 * branch)
    late = z >= 2
    rank = jnp.where(late, late_rank, early_rank)
    first = jnp.where(late, 2 * EARLY_UNITS + (z - 2) * LATE_UNITS, z * EARLY_UNITS)
    return first + rank, rank < jnp.where(late, LATE_UNITS, EARLY_UNITS)


def step_and_head(unit):
    step = (unit >= HEADS).astype(jnp.int32)
    return step, unit - step * HEADS


def far_to_near(k):
    return (0x36 >> (2 * k)) & 3


def column_code(i):
    return (far_to_near(i >> 2) << 4) + far_to_near(i & 3)


def for_places(planes, body):
    def across(i, carry):
        for plane in planes:
            run = functools.partial(body, i, column_code(i) + plane * 4)
            if plane == 0:
                pl.when(i < COLUMNS - 1)(run)
            else:
                run()
        return carry

    lax.fori_loop(0, COLUMNS, across, 0)


def stacked_heads(rows):
    return jnp.concatenate(
        [rows[:, h * HEAD_DIM : (h + 1) * HEAD_DIM] for h in range(HEADS)], axis=0
    )


def with_ones(values):
    return jnp.concatenate([values, jnp.ones_like(values)], axis=1)


def kernel(
    ts_hbm, gi_hbm, q_hbm, fresh_hbm, stale_hbm, out_ref,
    ts_ref, gi_ref, q_src, kv_src, pack, rx, scores_ref, o_buf, lse_buf, o_rx, lse_rx, own_all, own_fin,
    load_sem, kv_sem, q_sem, kv_send, q_send, o_send, lse_send, o_sem, lse_sem, own_send, own_sem,
):
    me = lax.axis_index("seq")
    branch = lax.axis_index("cfg")
    clip = lax.axis_index("clip")
    my_plane = (me >> 2) & 3
    my_slot = my_plane * COLUMNS + COLUMNS - 1
    unit, has_unit = unit_of(me, branch)
    unit_step, head = step_and_head(unit)
    half = (head >= HALF_HEADS).astype(jnp.int32)
    half_head = head - half * HALF_HEADS

    barrier = pltpu.get_barrier_semaphore()

    loads = [
        pltpu.make_async_copy(stale_hbm.at[0], kv_src.at[0], load_sem.at[0]),
        pltpu.make_async_copy(fresh_hbm.at[0, 0], kv_src.at[1], load_sem.at[1]),
        pltpu.make_async_copy(q_hbm.at[:, 0], q_src, load_sem.at[2]),
        pltpu.make_async_copy(fresh_hbm.at[1, 0], kv_src.at[2], load_sem.at[3]),
        pltpu.make_async_copy(ts_hbm, ts_ref, load_sem.at[4]),
        pltpu.make_async_copy(gi_hbm, gi_ref, load_sem.at[5]),
    ]
    pl.semaphore_signal(barrier, inc=1, device_id=(me, 1 - branch, clip), device_id_type=MESH)

    @pl.when(has_unit)
    def _():
        def greet(i, code):
            pl.semaphore_signal(
                barrier, inc=1, device_id=(me ^ code, branch, clip), device_id_type=MESH
            )

        for_places((FAR_PLANE,), greet)
        for_places(NEAR_PLANES, greet)

    for load in loads:
        load.start()

    for load in loads[:3]:
        load.wait()
    for step in range(STEPS):
        for h in range(HEADS):
            lanes = pl.ds(h * HEAD_DIM, HEAD_DIM)
            pack[step * HEADS + h, 0] = q_src[step, :, lanes]
            pack[step * HEADS + h, 1] = kv_src[step, 0, :, lanes]
            pack[step * HEADS + h, 2] = kv_src[step, 1, :, lanes]

    for load in loads[3:]:
        load.wait()

    rows = HEADS * TOK
    same_head = (
        lax.broadcasted_iota(jnp.int32, (rows, rows), 0) // TOK
        == lax.broadcasted_iota(jnp.int32, (rows, rows), 1) // TOK
    )
    for s in range(STEPS):
        scores = lax.dot_general(
            pack[pl.ds(s * HEADS, HEADS), 0].reshape(rows, HEAD_DIM),
            stacked_heads(kv_src[s + 1, 0]),
            (((1,), (1,)), ((), ())),
            preferred_element_type=jnp.float32,
        )
        scores = jnp.where(same_head, scores, MASKED)
        top = jnp.max(scores, axis=1, keepdims=True)
        weights = jnp.exp2((scores - top) * (SCORE_SCALE * LOG2E)).astype(jnp.bfloat16)
        summed = jnp.dot(
            weights, with_ones(stacked_heads(kv_src[s + 1, 1])), preferred_element_type=jnp.float32
        )
        totals = summed[:, HEAD_DIM:]
        own_all[:, s, 0] = (summed[:, :HEAD_DIM] / totals).reshape(2, rows // 2, HEAD_DIM)
        own_all[:, s, 1] = (top * SCORE_SCALE + jnp.log(totals)).reshape(2, rows // 2, HEAD_DIM)

    channel = (
        branch * (HALF_HEADS * HEAD_DIM)
        + lax.broadcasted_iota(jnp.int32, (HALF_HEADS, 1, HEAD_DIM), 0) * HEAD_DIM
        + lax.broadcasted_iota(jnp.int32, (HALF_HEADS, 1, HEAD_DIM), 2)
    ).astype(jnp.float32)
    frequency = jnp.exp(-math.log(1000.0) * channel / (HEADS * HEAD_DIM))
    gates = [
        1.0 + 0.5 * jnp.sin(ts_ref[s].astype(jnp.float32) * frequency) for s in range(STEPS)
    ]
    scale = 1.0 + 0.5 * gi_ref[0].astype(jnp.float32)

    pl.semaphore_wait(barrier, UNITS + 1 - has_unit.astype(jnp.int32))

    def slot_rows(slot):
        return pl.ds(pl.multiple_of(slot * TOK, TOK), TOK)

    def send_kv(i, code):
        u, held = unit_of(me ^ code, branch)

        @pl.when(held)
        def _():
            pltpu.make_async_remote_copy(
                src_ref=pack.at[u, pl.ds(1, 2)],
                dst_ref=rx.at[my_plane * COLUMNS + i, pl.ds(1, 2)],
                send_sem=kv_send,
                recv_sem=kv_sem,
                device_id=(me ^ code, branch, clip),
                device_id_type=MESH,
            ).start()

    def send_q(i, code):
        u, held = unit_of(me ^ code, branch)

        @pl.when(held)
        def _():
            pltpu.make_async_remote_copy(
                src_ref=pack.at[u, 0],
                dst_ref=rx.at[my_plane * COLUMNS + i, 0],
                send_sem=q_send,
                recv_sem=q_sem.at[my_plane],
                device_id=(me ^ code, branch, clip),
                device_id_type=MESH,
            ).start()

    @pl.when(my_plane == 0)
    def _():
        for_places((FAR_PLANE,), send_q)
        for_places(NEAR_PLANES, send_q)

    for_places((FAR_PLANE,), send_kv)
    for_places(NEAR_PLANES, send_kv)

    @pl.when(my_plane != 0)
    def _():
        for_places((FAR_PLANE,), send_q)
        for_places(NEAR_PLANES, send_q)

    @pl.when(has_unit)
    def _():
        pltpu.make_async_copy(pack.at[unit, pl.ds(1, 2)], rx.at[my_slot, pl.ds(1, 2)], kv_sem).start()
        pltpu.make_async_copy(pack.at[unit, 0], rx.at[my_slot, 0], q_sem.at[my_plane]).start()

    own_copy = pltpu.make_async_remote_copy(
        src_ref=own_all.at[1 - branch],
        dst_ref=own_fin.at[branch],
        send_sem=own_send,
        recv_sem=own_sem.at[0],
        device_id=(me, 1 - branch, clip),
        device_id_type=MESH,
    )
    own_copy.start()
    own_local = pltpu.make_async_copy(own_all.at[branch], own_fin.at[branch], own_sem.at[1])
    own_local.start()

    def send_out(slot, code):
        pltpu.make_async_remote_copy(
            src_ref=o_buf.at[slot_rows(slot), :],
            dst_ref=o_rx.at[branch, unit_step, half_head],
            send_sem=o_send,
            recv_sem=o_sem,
            device_id=(me ^ code, half, clip),
            device_id_type=MESH,
        ).start()
        pltpu.make_async_remote_copy(
            src_ref=lse_buf.at[slot],
            dst_ref=lse_rx.at[branch, unit_step, half_head],
            send_sem=lse_send,
            recv_sem=lse_sem,
            device_id=(me ^ code, half, clip),
            device_id_type=MESH,
        ).start()

    def for_chunk(c):
        away = my_plane ^ c

        def send_slots(k, carry):
            for m in range(3):
                i = 3 * k + m
                send_out(c * COLUMNS + i, column_code(i) + away * 4)
            return carry

        lax.fori_loop(0, (COLUMNS - 1) // 3, send_slots, 0)

        @pl.when(away != 0)
        def _():
            send_out(c * COLUMNS + COLUMNS - 1, away * 4)

    @pl.when(has_unit)
    def _():
        kv_all = rx.at[:, pl.ds(1, 2)]
        pltpu.make_async_copy(kv_all, kv_all, kv_sem).wait()
        lane_token = lax.broadcasted_iota(jnp.int32, (1, TOK, HEAD_DIM), 2) % TOK
        picked = lane_token == lax.broadcasted_iota(jnp.int32, (1, TOK, HEAD_DIM), 1)
        same_patch = (
            lax.broadcasted_iota(jnp.int32, (CHUNK, CHUNK), 0) // TOK
            == lax.broadcasted_iota(jnp.int32, (CHUNK, CHUNK), 1) // TOK
        )
        for c in range(PLANES):
            slots, here = pl.ds(c * COLUMNS, COLUMNS), pl.ds(c * CHUNK, CHUNK)
            q_chunk = rx.at[slots, 0]
            pltpu.make_async_copy(q_chunk, q_chunk, q_sem.at[c]).wait()
            scores_ref[...] = lax.dot_general(
                q_chunk[...].reshape(CHUNK, HEAD_DIM),
                rx[:, 1].reshape(SEQ_TOKENS, HEAD_DIM),
                (((1,), (1,)), ((), ())),
                preferred_element_type=jnp.float32,
            )
            scores_ref[:, here] = jnp.where(same_patch, MASKED, scores_ref[:, here])
            scores = scores_ref[...]
            top = jnp.max(scores, axis=1, keepdims=True)
            weights = jnp.exp2((scores - top) * (SCORE_SCALE * LOG2E)).astype(jnp.bfloat16)
            summed = jnp.dot(weights, with_ones(rx[:, 2].reshape(SEQ_TOKENS, HEAD_DIM)), preferred_element_type=jnp.float32)
            totals = summed[:, HEAD_DIM:]
            o_buf[here, :] = (summed[:, :HEAD_DIM] / totals).astype(jnp.bfloat16)
            lse = (top * SCORE_SCALE + jnp.log(totals)).reshape(COLUMNS, TOK, HEAD_DIM)
            lse_buf[slots] = jnp.sum(
                jnp.where(picked, lse, 0.0), axis=1, keepdims=True
            )
            for_chunk(c)

        @pl.when(half == branch)
        def _():
            pltpu.make_async_copy(
                o_buf.at[slot_rows(my_slot), :], o_rx.at[branch, unit_step, half_head], o_sem
            ).start()
            pltpu.make_async_copy(
                lse_buf.at[my_slot], lse_rx.at[branch, unit_step, half_head], lse_sem
            ).start()

        @pl.when(half != branch)
        def _():
            send_out(my_slot, 0)

    own_copy.wait_recv()
    own_local.wait()
    pltpu.make_async_copy(lse_rx, lse_rx, lse_sem).wait()
    pltpu.make_async_copy(o_rx, o_rx, o_sem).wait()

    token = lax.broadcasted_iota(jnp.int32, (1, TOK, HEAD_DIM), 1)
    lane = lax.broadcasted_iota(jnp.int32, (1, TOK, HEAD_DIM), 2)

    def attended(b, s):
        remote = o_rx[b, s].astype(jnp.float32)
        remote_lse = jnp.sum(jnp.where(token == lane, lse_rx[b, s], 0.0), axis=2, keepdims=True)
        own = own_fin[b, s, 0].reshape(HALF_HEADS, TOK, HEAD_DIM)
        own_lse = own_fin[b, s, 1].reshape(HALF_HEADS, TOK, HEAD_DIM)
        share = 1.0 / (1.0 + jnp.exp(own_lse - remote_lse))
        return own + share * (remote - own)

    for s in range(STEPS):
        cond = attended(0, s)
        uncond = attended(1, s)
        guided = (gates[s] * (uncond + scale * (cond - uncond))).astype(jnp.bfloat16)
        for h in range(HALF_HEADS):
            out_ref[s, :, h * HEAD_DIM : (h + 1) * HEAD_DIM] = guided[h]

    def wait_sent(count):
        kv_sent, q_sent = pack.at[pl.ds(0, count), pl.ds(1, 2)], pack.at[pl.ds(0, count), 0]
        pltpu.make_async_copy(kv_sent, kv_sent, kv_send).wait()
        pltpu.make_async_copy(q_sent, q_sent, q_send).wait()

    own_copy.wait_send()

    @pl.when(has_unit)
    def _():
        wait_sent(UNITS - 1)

        @pl.when(half == branch)
        def _():
            out_rows, lse_rows = pl.ds(0, SEQ_TOKENS - TOK), pl.ds(0, N_SEQ - 1)
            pltpu.make_async_copy(o_buf.at[out_rows], o_buf.at[out_rows], o_send).wait()
            pltpu.make_async_copy(lse_buf.at[lse_rows], lse_buf.at[lse_rows], lse_send).wait()

        @pl.when(half != branch)
        def _():
            pltpu.make_async_copy(o_buf, o_buf, o_send).wait()
            pltpu.make_async_copy(lse_buf, lse_buf, lse_send).wait()

    @pl.when(jnp.logical_not(has_unit))
    def _():
        wait_sent(UNITS)


def shards(queries, fresh_kv, stale_kv, timesteps, guidance_index):
    bf16, f32 = jnp.bfloat16, jnp.float32
    rows = HALF_HEADS * TOK
    dma = pltpu.SemaphoreType.DMA
    return pl.pallas_call(
        kernel,
        out_shape=jax.ShapeDtypeStruct((STEPS, TOK, HALF_HEADS * HEAD_DIM), bf16),
        in_specs=[pl.BlockSpec(memory_space=pltpu.HBM)] * 5,
        out_specs=pl.BlockSpec(memory_space=pltpu.VMEM),
        scratch_shapes=[
            pltpu.SMEM((STEPS,), jnp.int32),
            pltpu.SMEM((1,), jnp.int32),
            pltpu.VMEM((STEPS, TOK, HEADS * HEAD_DIM), bf16),
            pltpu.VMEM((STEPS + 1, 2, TOK, HEADS * HEAD_DIM), bf16),
            pltpu.VMEM((UNITS, 3, TOK, HEAD_DIM), bf16),
            pltpu.VMEM((N_SEQ, 3, TOK, HEAD_DIM), bf16),
            pltpu.VMEM((CHUNK, SEQ_TOKENS), f32),
            pltpu.VMEM((SEQ_TOKENS, HEAD_DIM), bf16),
            pltpu.VMEM((N_SEQ, 1, HEAD_DIM), f32),
            pltpu.VMEM((2, STEPS, HALF_HEADS, TOK, HEAD_DIM), bf16),
            pltpu.VMEM((2, STEPS, HALF_HEADS, 1, HEAD_DIM), f32),
            pltpu.VMEM((2, STEPS, 2, rows, HEAD_DIM), f32),
            pltpu.VMEM((2, STEPS, 2, rows, HEAD_DIM), f32),
            dma((6,)), dma, dma((PLANES,)),
            dma, dma, dma, dma,
            dma, dma, dma, dma((2,)),
        ],
        compiler_params=pltpu.CompilerParams(
            collective_id=0, has_side_effects=True, vmem_limit_bytes=VMEM_GRANT
        ),
        name="patch_attention",
    )(timesteps, guidance_index, queries, fresh_kv, stale_kv)


def solution(mesh):
    in_specs = (
        P(None, "cfg", ("clip", "seq"), None),
        P(None, "cfg", None, ("clip", "seq"), None),
        P("cfg", None, ("clip", "seq"), None),
        P(),
        P(),
    )
    out_specs = P(None, ("clip", "seq"), "cfg")
    return jax.shard_map(shards, mesh=mesh, in_specs=in_specs, out_specs=out_specs, check_vma=False)
```
